512 devices in a mesh: space: 128 (over z, x, core), blk: 4 (over y).
Axes of the slice: x: 4, y: 4, z: 16, core: 2. Of those that a mesh axis runs over, the one named last changes fastest.
Arguments:
- pressure: float32 [512, 262144], P('blk', 'space'), may hold values from -6 to 6
- final_steps: float32 [128, 262144], P(None, 'space'), may hold values from -6 to 6
- weights: float32 [262144], P('space'), may hold values from 0.5 to 4.5, as said below
Outputs:
- spectra: bfloat16 [4, 128, 2, 262144], P(None, 'blk', None, 'space')
- csd: float32 [2, 128, 4, 4], P(None, 'blk')
The draws below stay inside these ranges and needn't reach their ends.
Inputs may be any that keep to these rules, and one draw needn't show every extreme that they name: Positive weights.
All inputs are finite; a program needn't handle non-finite values.
Results may differ from the reference program's by a relative error of at most 0.0055.
Values may be sent and summed in bfloat16 or wider, within the bound.
No kernel may reach another device: no remote copies, remote signals or barrier semaphores. Data moves between devices by JAX's collectives and lax.ppermute only.
A program may use at most 64 MiB of HBM per device.

```python
import math
import jax
import jax.numpy as jnp
from jax import lax

HOP = 128
BLEN = 256
NFREQ = 128
BLOCKS = 4
NPTS = 262144


def draw_weights(key, part):
    key = jax.random.fold_in(key, 7)
    ramp = 1.0 + 2.0 * jnp.arange(NPTS, dtype=jnp.float32) / NPTS
    spread = jax.random.uniform(key, (NPTS,), jnp.float32, 0.5, 1.5)
    return ramp * spread


def levels(own_key, dims, shards, least, top_value):
    level, own = 1.0, jax.random.fold_in(own_key, 6)
    for axis_at, shards_of in shards:
        heights = jnp.exp(jax.random.uniform(jax.random.fold_in(own, axis_at), (shards_of,), jnp.float32, least / len(shards), top_value / len(shards)))
        level = level * jnp.repeat(heights, dims[axis_at] // shards_of).reshape([-1 if axis == axis_at else 1 for axis in range(len(dims))])
    return level


def noise(own_key, shape, scale, most, split=(), kind=jnp.bfloat16):
    factor_of = levels(own_key, shape, split, -0.22, 0.18) if split else 1.0
    values = jax.random.normal(own_key, shape, jnp.float32) * scale * factor_of
    return jnp.minimum(jnp.maximum(values, -most), most).astype(kind)


def setup_inputs(seed: int = 0) -> dict:
    keys = jax.random.split(jax.random.key(seed), 4)
    return {
        "pressure": noise(keys[0], (BLOCKS * HOP, NPTS), 1.0, 6.0, ((0, 4), (1, 128)), jnp.float32),
        "final_steps": noise(keys[1], (HOP, NPTS), 1.0, 6.0, ((1, 128),), jnp.float32),
        "weights": draw_weights(jax.random.fold_in(keys[3], 71), 0),
    }


def make_table(blen, nfreq):
    t = jnp.arange(blen, dtype=jnp.int32)
    k = jnp.arange(nfreq, dtype=jnp.int32)
    phase = k[:, None] * t[None, :] % blen
    angle = 2.0 * math.pi / blen * phase.astype(jnp.float32)
    scale = 1.0 / math.sqrt(3.0 * blen / 8.0)
    table = jnp.stack([jnp.cos(angle) * scale, -jnp.sin(angle) * scale], axis=1)
    return table.reshape(2 * nfreq, blen).astype(jnp.bfloat16)

def make_hann(blen):
    t = jnp.arange(blen, dtype=jnp.float32)
    return 0.5 - 0.5 * jnp.cos(2.0 * math.pi / blen * t)

def cross_sums(spectra, weights, count):
    values = spectra.astype(jnp.float32)
    real_part = values[:, :, 0]
    imag_part = values[:, :, 1]
    high = lax.Precision.HIGHEST
    real_w = real_part * weights
    imag_w = imag_part * weights
    first = jnp.einsum('ikn,jkn->kij', real_w, real_part, precision=high) + jnp.einsum('ikn,jkn->kij', imag_w, imag_part, precision=high)
    second = jnp.einsum('ikn,jkn->kij', imag_w, real_part, precision=high) - jnp.einsum('ikn,jkn->kij', real_w, imag_part, precision=high)
    return jnp.stack([first, second], axis=0) / count

def reference(pressure, final_steps, weights):
    total = lax.optimization_barrier(jnp.sum(pressure, axis=0)) + lax.optimization_barrier(jnp.sum(final_steps, axis=0))
    mean = total / (HOP * (BLOCKS + 1))
    full = jnp.concatenate([pressure, final_steps], axis=0) - mean
    table = make_table(BLEN, NFREQ)
    hann = make_hann(BLEN)
    blocks = []
    for index in range(BLOCKS):
        piece = full[index * HOP:index * HOP + BLEN]
        windowed = (piece * hann[:, None]).astype(jnp.bfloat16)
        coeff = jnp.dot(table, windowed, preferred_element_type=jnp.float32).astype(jnp.bfloat16)
        blocks.append(coeff.reshape(NFREQ, 2, NPTS))
    spectra = jnp.stack(blocks, axis=0)
    csd = cross_sums(spectra, weights, float(NPTS))
    return (spectra, csd)
```

```python
import math

import jax
import jax.numpy as jnp
from jax import lax
from jax.sharding import Mesh
from jax.sharding import PartitionSpec as P

HOP = 128
SPACE = ("z", "x", "core")


def summed_over(value, axes):
    count = lax.axis_size(axes)
    sent = jnp.broadcast_to(value[None], (count, *value.shape))
    return jnp.sum(lax.all_to_all(sent, axes, 0, 0, tiled=True), axis=0)


def passed_along(value, axis, steps):
    count = lax.axis_size(axis)
    leading, last = (max(0, -steps), min(count, count - steps))
    return lax.ppermute(value, axis, [(source, source + steps) for source in range(leading, last)])


def make_table(blen, nfreq):
    t = jnp.arange(blen, dtype=jnp.int32)
    k = jnp.arange(nfreq, dtype=jnp.int32)
    phase = k[:, None] * t[None, :] % blen
    angle = 2.0 * math.pi / blen * phase.astype(jnp.float32)
    scale = 1.0 / math.sqrt(3.0 * blen / 8.0)
    table = jnp.stack([jnp.cos(angle) * scale, -jnp.sin(angle) * scale], axis=1)
    return table.reshape(2 * nfreq, blen).astype(jnp.bfloat16)


def make_hann(blen):
    t = jnp.arange(blen, dtype=jnp.float32)
    return 0.5 - 0.5 * jnp.cos(2.0 * math.pi / blen * t)


def cross_sums(spectra, weights, count):
    values = spectra.astype(jnp.float32)
    real_part = values[:, :, 0]
    imag_part = values[:, :, 1]
    high = lax.Precision.HIGHEST
    real_w = real_part * weights
    imag_w = imag_part * weights
    first = jnp.einsum("ikn,jkn->kij", real_w, real_part, precision=high) + jnp.einsum(
        "ikn,jkn->kij", imag_w, imag_part, precision=high
    )
    second = jnp.einsum("ikn,jkn->kij", imag_w, real_part, precision=high) - jnp.einsum(
        "ikn,jkn->kij", real_w, imag_part, precision=high
    )
    return jnp.stack([first, second], axis=0) / count


def local(pressure, final_steps, weights):
    blocks_count = lax.axis_size("blk")
    position = lax.axis_index("blk")
    is_last = position == blocks_count - 1
    points = pressure.shape[1]
    own_sum = jnp.sum(pressure, axis=0) + jnp.where(is_last, jnp.sum(final_steps, axis=0), 0.0)
    total = lax.psum(own_sum, "blk")
    mean = total / (HOP * (blocks_count + 1))
    blen = 2 * HOP
    hann = make_hann(blen)
    table = make_table(blen, HOP)
    following = passed_along(pressure, "blk", -1)
    following = jnp.where(is_last, final_steps, following)
    segment = jnp.concatenate([pressure, following], axis=0) - mean
    windowed = (segment * hann[:, None]).astype(jnp.bfloat16)
    coeff = jnp.dot(table, windowed, preferred_element_type=jnp.float32).astype(jnp.bfloat16)
    coeff = coeff.reshape(1, HOP, 2, points)
    spectra = lax.all_to_all(coeff, "blk", split_axis=1, concat_axis=0, tiled=True)
    partial_sums = cross_sums(spectra, weights, float(points * lax.axis_size(SPACE)))
    flat = jnp.transpose(partial_sums, (0, 2, 3, 1)).reshape(-1)
    flat = summed_over(summed_over(flat, ("x", "core")), ("z",))
    csd = jnp.transpose(flat.reshape(2, blocks_count, blocks_count, -1), (0, 3, 1, 2))
    return (spectra, csd)


def solution(mesh):
    split = Mesh(mesh.devices.reshape(-1, 4, 2, mesh.shape["blk"]), (*SPACE, "blk"))
    return jax.shard_map(
        local,
        mesh=split,
        in_specs=(P("blk", SPACE), P(None, SPACE), P(SPACE)),
        out_specs=(P(None, "blk", None, SPACE), P(None, "blk", None, None)),
        check_vma=False,
    )
```

```python
import math

import jax
import jax.numpy as jnp
import numpy as np
from jax import lax
from jax.experimental import pallas as pl
from jax.experimental.pallas import tpu as pltpu
from jax.sharding import Mesh
from jax.sharding import PartitionSpec as P

HOP = 128
BLEN = 2 * HOP
BLOCKS = 4
SPACE = ("z", "x", "core")
LIMIT = 48 * 1024 * 1024
MEANS = 16
PAIRS = [(i, j) for i in range(BLOCKS) for j in range(i, BLOCKS)]
CROSS = [(i, j) for i, j in PAIRS if i < j]
SUMS = len(PAIRS) + len(CROSS)

VMEM = pl.BlockSpec(memory_space=pltpu.VMEM)
SMEM = pl.BlockSpec(memory_space=pltpu.SMEM)


def tables():
    t = np.arange(BLEN)
    k = np.arange(HOP)
    angle = 2.0 * math.pi / BLEN * (k[:, None] * t[None, :] % BLEN)
    scale = 1.0 / math.sqrt(3.0 * BLEN / 8.0)
    parts = np.stack([np.cos(angle) * scale, -np.sin(angle) * scale], axis=1)
    hann = 0.5 - 0.5 * np.cos(2.0 * math.pi / BLEN * t)
    return (
        jnp.asarray(parts.reshape(2 * HOP, BLEN), jnp.bfloat16),
        jnp.asarray(parts.swapaxes(0, 1).reshape(2 * HOP, BLEN), jnp.bfloat16),
        jnp.asarray(np.repeat(hann[:, None], 128, axis=1), jnp.float32),
    )


def split_kernel(pressure_ref, out_ref):
    width = out_ref.shape[2]
    for quarter in range(BLOCKS):
        x = pressure_ref[:, quarter * width : (quarter + 1) * width]
        mean = jnp.sum(x, axis=0, keepdims=True) * (1.0 / HOP)
        out_ref[quarter, :HOP] = (x - mean).astype(jnp.bfloat16)
        high = mean.astype(jnp.bfloat16).astype(jnp.float32)
        middle = (mean - high).astype(jnp.bfloat16).astype(jnp.float32)
        low = mean - high - middle
        row = lax.broadcasted_iota(jnp.int32, (MEANS, width), 0)
        rows = jnp.where(row == 0, high, jnp.where(row == 1, middle, jnp.where(row == 2, low, 0.0)))
        out_ref[quarter, HOP:] = rows.astype(jnp.bfloat16)


def spectra_kernel(
    count, pos_ref, got_ref, final_ref, weights_ref, table_ref, split_ref, hann_ref,
    piece0, piece1, piece2, piece3, csd_ref, rotated, coeff, sums,
):
    me = pos_ref[0]
    width = got_ref.shape[2]
    own = pl.ds(pl.multiple_of(me * width, width), width)
    group = 2 * HOP // BLOCKS
    for step in range(BLOCKS):
        rows = pl.multiple_of(lax.rem(me + step, BLOCKS) * group, group)
        rotated[step * group : (step + 1) * group] = table_ref[pl.ds(rows, group), :]

    final = final_ref[:, own]
    means = [
        jnp.sum(got_ref[s, HOP:].astype(jnp.float32), axis=0, keepdims=True) for s in range(BLOCKS)
    ]
    total = jnp.sum(final, axis=0, keepdims=True) + HOP * (means[0] + means[1] + means[2] + means[3])
    mean = total / (HOP * (BLOCKS + 1))
    hann = jnp.concatenate([hann_ref[...]] * (width // 128), axis=1)

    def segment(s):
        if s == BLOCKS:
            return final - mean
        return got_ref[s, :HOP].astype(jnp.float32) + (means[s] - mean)

    for b in range(BLOCKS):
        windowed = jnp.concatenate([segment(b) * hann[:HOP], segment(b + 1) * hann[HOP:]], axis=0)
        windowed = windowed.astype(jnp.bfloat16)
        mixed = jnp.dot(rotated[...], windowed, preferred_element_type=jnp.float32)
        mixed = mixed.astype(jnp.bfloat16)
        for step, piece in enumerate((piece0, piece1, piece2, piece3)):
            piece[b] = mixed[step * group : (step + 1) * group]
        apart = jnp.dot(split_ref[...], windowed, preferred_element_type=jnp.float32)
        coeff[b] = apart.astype(jnp.bfloat16).astype(jnp.float32)

    weights = weights_ref[:, own] * (1.0 / count)
    freqs = HOP // BLOCKS

    def tile(t, carry):
        at = pl.multiple_of(t * 8, 8)
        acc = [None] * SUMS
        for lane in range(0, width, 128):
            cols = slice(lane, lane + 128)
            w = weights[:, cols]
            re = [coeff[b, pl.ds(at, 8), cols] for b in range(BLOCKS)]
            im = [coeff[b, pl.ds(at + HOP, 8), cols] for b in range(BLOCKS)]
            re_w = [v * w for v in re]
            im_w = [v * w for v in im]
            terms = [re_w[i] * re[j] + im_w[i] * im[j] for i, j in PAIRS]
            terms += [im_w[i] * re[j] - re_w[i] * im[j] for i, j in CROSS]
            acc = [v if a is None else a + v for a, v in zip(acc, terms)]
        first = (t // (freqs // 8)) * (SUMS * freqs) + lax.rem(t, freqs // 8) * 8
        for p in range(SUMS):
            sums[pl.ds(pl.multiple_of(first + p * freqs, 8), 8), :] = acc[p]
        return carry

    lax.fori_loop(0, HOP // 8, tile, 0)
    values = sums[...]
    high = values.astype(jnp.bfloat16)
    low = (values - high.astype(jnp.float32)).astype(jnp.bfloat16)
    ones = jnp.ones((8, 128), jnp.bfloat16)
    along = (((1,), (1,)), ((), ()))
    lanes = lax.dot_general(ones, high, along, preferred_element_type=jnp.float32)
    lanes += lax.dot_general(ones, low, along, preferred_element_type=jnp.float32)
    part = SUMS * freqs
    for q in range(BLOCKS):
        csd_ref[q * 8 : (q + 1) * 8] = lanes[:, q * part : (q + 1) * part]


def join_kernel(pos_ref, piece0, piece1, piece2, piece3, out_ref):
    me = pos_ref[0]
    width = piece0.shape[2]
    for step, piece in enumerate((piece0, piece1, piece2, piece3)):
        source = lax.rem(me + BLOCKS - step, BLOCKS)
        out_ref[:, :, pl.ds(pl.multiple_of(source * width, width), width)] = piece[...]


def summed_over(value, axes):
    size = lax.axis_size(axes)
    sent = jnp.broadcast_to(value[None], (size, *value.shape))
    return jnp.sum(lax.all_to_all(sent, axes, 0, 0, tiled=True), axis=0)


def local(pressure, final_steps, weights):
    points = pressure.shape[1]
    width = points // BLOCKS
    freqs = HOP // BLOCKS
    position = lax.axis_index("blk").astype(jnp.int32).reshape(1)
    params = pltpu.CompilerParams(vmem_limit_bytes=LIMIT)
    sent = pl.pallas_call(
        split_kernel,
        out_shape=jax.ShapeDtypeStruct((BLOCKS, HOP + MEANS, width), jnp.bfloat16),
        in_specs=[VMEM],
        out_specs=VMEM,
        compiler_params=params,
    )(pressure)
    got = lax.all_to_all(sent, "blk", 0, 0, tiled=True)
    table, split, hann = tables()
    count = float(points * lax.axis_size(SPACE))
    piece = jax.ShapeDtypeStruct((BLOCKS, 2 * freqs, width), jnp.bfloat16)
    group = lax.axis_size(("blk", "x", "core"))
    *pieces, partial_sums = pl.pallas_call(
        lambda *refs: spectra_kernel(count, *refs),
        out_shape=[piece] * BLOCKS + [jax.ShapeDtypeStruct((8 * BLOCKS, SUMS * freqs), jnp.float32)],
        in_specs=[SMEM] + [VMEM] * 6,
        out_specs=[VMEM] * 5,
        scratch_shapes=[
            pltpu.VMEM((2 * HOP, BLEN), jnp.bfloat16),
            pltpu.VMEM((BLOCKS, 2 * HOP, width), jnp.float32),
            pltpu.VMEM((SUMS * HOP, 128), jnp.float32),
        ],
        compiler_params=params,
    )(position, got, final_steps, weights.reshape(1, points), table, split, hann)
    partial_sums = partial_sums.reshape(BLOCKS, 8, -1)[:, : group // BLOCKS].reshape(group, -1)
    partial_sums = jnp.sum(
        lax.all_to_all(partial_sums, ("blk", "x", "core"), 0, 0, tiled=True), axis=0
    )
    moved = [
        lax.ppermute(value, "blk", [(i, (i + step) % BLOCKS) for i in range(BLOCKS)]) if step else value
        for step, value in enumerate(pieces)
    ]
    spectra = pl.pallas_call(
        join_kernel,
        out_shape=jax.ShapeDtypeStruct((BLOCKS, 2 * freqs, points), jnp.bfloat16),
        in_specs=[SMEM] + [VMEM] * BLOCKS,
        out_specs=VMEM,
        compiler_params=params,
    )(position, *moved)
    spectra = spectra.reshape(BLOCKS, freqs, 2, points)
    rows = summed_over(partial_sums, ("z",)).reshape(SUMS, freqs)
    zero = jnp.zeros_like(rows[0])
    both = []
    for i in range(BLOCKS):
        both += [rows[PAIRS.index((min(i, j), max(i, j)))] for j in range(BLOCKS)]
    for i in range(BLOCKS):
        for j in range(BLOCKS):
            at = len(PAIRS) + (CROSS.index((min(i, j), max(i, j))) if i != j else 0)
            both.append(zero if i == j else rows[at] if i < j else -rows[at])
    csd = jnp.stack(both).reshape(2, BLOCKS, BLOCKS, freqs)
    return (spectra, jnp.transpose(csd, (0, 3, 1, 2)))


def solution(mesh):
    across = min(4, mesh.shape["space"] // 2)
    split = Mesh(mesh.devices.reshape(-1, across, 2, mesh.shape["blk"]), (*SPACE, "blk"))
    return jax.shard_map(
        local,
        mesh=split,
        in_specs=(P("blk", SPACE), P(None, SPACE), P(SPACE)),
        out_specs=(P(None, "blk", None, SPACE), P(None, "blk", None, None)),
        check_vma=False,
    )
```

```python
import functools
import math

import jax
import jax.numpy as jnp
import numpy as np
from jax import lax
from jax.experimental import pallas as pl
from jax.experimental.pallas import tpu as pltpu
from jax.sharding import Mesh
from jax.sharding import PartitionSpec as P

HOP = 128
BLEN = 2 * HOP
BLOCKS = 4
SPACE = ("z", "x", "core")
LIMIT = 48 * 1024 * 1024
WAIT = pl.CostEstimate(flops=10**10, bytes_accessed=10**10, transcendentals=0)
MEANS = 16
PAIRS = [(i, j) for i in range(BLOCKS) for j in range(i, BLOCKS)]
CROSS = [(i, j) for i, j in PAIRS if i < j]
SUMS = len(PAIRS) + len(CROSS)

VMEM = pl.BlockSpec(memory_space=pltpu.VMEM)
SMEM = pl.BlockSpec(memory_space=pltpu.SMEM)
HBM = pl.BlockSpec(memory_space=pltpu.HBM)


def tables():
    t = np.arange(BLEN)
    k = np.arange(HOP)
    angle = 2.0 * math.pi / BLEN * (k[:, None] * t[None, :] % BLEN)
    scale = 1.0 / math.sqrt(3.0 * BLEN / 8.0)
    parts = np.stack([np.cos(angle) * scale, -np.sin(angle) * scale], axis=1)
    hann = 0.5 - 0.5 * np.cos(2.0 * math.pi / BLEN * t)
    return (
        jnp.asarray(parts.reshape(2 * HOP, BLEN), jnp.bfloat16),
        jnp.asarray(parts.swapaxes(0, 1).reshape(2 * HOP, BLEN), jnp.bfloat16),
        jnp.asarray(np.repeat(hann[:, None], 128, axis=1), jnp.float32),
    )


def split_kernel(pressure_ref, out_ref, held, ready, sem_in, sem_out):
    width = out_ref.shape[2]

    def fetch(quarter):
        cols = slice(quarter * width, (quarter + 1) * width)
        return pltpu.make_async_copy(pressure_ref.at[:, cols], held.at[quarter], sem_in.at[quarter])

    def store(quarter):
        return pltpu.make_async_copy(ready.at[quarter], out_ref.at[quarter], sem_out.at[quarter])

    for quarter in range(BLOCKS):
        fetch(quarter).start()
    for quarter in range(BLOCKS):
        fetch(quarter).wait()
        x = held[quarter]
        mean = jnp.sum(x, axis=0, keepdims=True) * (1.0 / HOP)
        ready[quarter, :HOP] = (x - mean).astype(jnp.bfloat16)
        high = mean.astype(jnp.bfloat16).astype(jnp.float32)
        middle = (mean - high).astype(jnp.bfloat16).astype(jnp.float32)
        low = mean - high - middle
        row = lax.broadcasted_iota(jnp.int32, (MEANS, width), 0)
        rows = jnp.where(row == 0, high, jnp.where(row == 1, middle, jnp.where(row == 2, low, 0.0)))
        ready[quarter, HOP:] = rows.astype(jnp.bfloat16)
        store(quarter).start()
    for quarter in range(BLOCKS):
        store(quarter).wait()


def sums_kernel(
    count, pos_ref, got_ref, final_ref, weights_ref, table_ref, hann_ref, windowed_ref, csd_ref, coeff, sums
):
    me = pos_ref[0]
    width = got_ref.shape[2]
    own = pl.ds(pl.multiple_of(me * width, width), width)
    final = final_ref[:, own]
    means = [
        jnp.sum(got_ref[s, HOP:].astype(jnp.float32), axis=0, keepdims=True) for s in range(BLOCKS)
    ]
    total = jnp.sum(final, axis=0, keepdims=True) + HOP * (means[0] + means[1] + means[2] + means[3])
    mean = total / (HOP * (BLOCKS + 1))
    hann = jnp.concatenate([hann_ref[...]] * (width // 128), axis=1)

    def segment(s):
        if s == BLOCKS:
            return final - mean
        return got_ref[s, :HOP].astype(jnp.float32) + (means[s] - mean)

    for b in range(BLOCKS):
        windowed = jnp.concatenate([segment(b) * hann[:HOP], segment(b + 1) * hann[HOP:]], axis=0)
        windowed = windowed.astype(jnp.bfloat16)
        windowed_ref[b] = windowed
        apart = jnp.dot(table_ref[...], windowed, preferred_element_type=jnp.float32)
        coeff[b] = apart.astype(jnp.bfloat16).astype(jnp.float32)

    weights = weights_ref[:, own] * (1.0 / count)
    freqs = HOP // BLOCKS

    def tile(t, carry):
        at = pl.multiple_of(t * 8, 8)
        acc = [None] * SUMS
        for lane in range(0, width, 128):
            cols = slice(lane, lane + 128)
            w = weights[:, cols]
            re = [coeff[b, pl.ds(at, 8), cols] for b in range(BLOCKS)]
            im = [coeff[b, pl.ds(at + HOP, 8), cols] for b in range(BLOCKS)]
            re_w = [v * w for v in re]
            im_w = [v * w for v in im]
            terms = [re_w[i] * re[j] + im_w[i] * im[j] for i, j in PAIRS]
            terms += [im_w[i] * re[j] - re_w[i] * im[j] for i, j in CROSS]
            acc = [v if a is None else a + v for a, v in zip(acc, terms)]
        first = (t // (freqs // 8)) * (SUMS * freqs) + lax.rem(t, freqs // 8) * 8
        for p in range(SUMS):
            sums[pl.ds(pl.multiple_of(first + p * freqs, 8), 8), :] = acc[p]
        return carry

    lax.fori_loop(0, HOP // 8, tile, 0)
    values = sums[...]
    high = values.astype(jnp.bfloat16)
    low = (values - high.astype(jnp.float32)).astype(jnp.bfloat16)
    ones = jnp.ones((8, 128), jnp.bfloat16)
    along = (((1,), (1,)), ((), ()))
    lanes = lax.dot_general(ones, high, along, preferred_element_type=jnp.float32)
    lanes += lax.dot_general(ones, low, along, preferred_element_type=jnp.float32)
    part = SUMS * freqs
    copies = csd_ref.shape[0] // BLOCKS
    for q in range(BLOCKS):
        for copy in range(copies):
            csd_ref[q * copies + copy] = lanes[:1, q * part : (q + 1) * part]


def spectra_kernel(pos_ref, windowed_ref, table_ref, piece0, piece1, piece2, piece3, rotated):
    me = pos_ref[0]
    group = 2 * HOP // BLOCKS
    for step in range(BLOCKS):
        rows = pl.multiple_of(lax.rem(me + step, BLOCKS) * group, group)
        rotated[step * group : (step + 1) * group] = table_ref[pl.ds(rows, group), :]
    for b in range(BLOCKS):
        mixed = jnp.dot(rotated[...], windowed_ref[b], preferred_element_type=jnp.float32)
        mixed = mixed.astype(jnp.bfloat16)
        for step, piece in enumerate((piece0, piece1, piece2, piece3)):
            piece[b] = mixed[step * group : (step + 1) * group]


def repeat_kernel(got_ref, out_ref):
    value = jnp.sum(got_ref[...], axis=0)
    for copy in range(out_ref.shape[0]):
        out_ref[copy] = value


def join_kernel(pos_ref, piece0, piece1, piece2, piece3, out_ref):
    me = pos_ref[0]
    width = piece0.shape[2]
    for step, piece in enumerate((piece0, piece1, piece2, piece3)):
        source = lax.rem(me + BLOCKS - step, BLOCKS)
        out_ref[:, :, pl.ds(pl.multiple_of(source * width, width), width)] = piece[...]


def matrix_kernel(got_ref, spectra_ref, csd_ref):
    freqs = csd_ref.shape[2]
    total = jnp.sum(got_ref[...], axis=0)
    rows = [total[:, p * freqs : (p + 1) * freqs] for p in range(SUMS)]
    for i in range(BLOCKS):
        for j in range(BLOCKS):
            pair = (min(i, j), max(i, j))
            csd_ref[i, j : j + 1] = rows[PAIRS.index(pair)]
            if i == j:
                csd_ref[BLOCKS + i, j : j + 1] = jnp.zeros_like(total[:, :freqs])
            else:
                cross = rows[len(PAIRS) + CROSS.index(pair)]
                csd_ref[BLOCKS + i, j : j + 1] = cross if i < j else -cross


def call(kernel, out, operands, scratch=(), cost=None):
    specs = [o[1] if isinstance(o, tuple) else VMEM for o in operands]
    return pl.pallas_call(
        kernel,
        out_shape=out,
        in_specs=specs,
        out_specs=jax.tree.map(lambda _: VMEM, out),
        scratch_shapes=scratch,
        compiler_params=pltpu.CompilerParams(vmem_limit_bytes=LIMIT),
        cost_estimate=cost,
    )(*[o[0] if isinstance(o, tuple) else o for o in operands])


def local(pressure, final_steps, weights):
    points = pressure.shape[1]
    width = points // BLOCKS
    freqs = HOP // BLOCKS
    here = (lax.axis_index("blk").astype(jnp.int32).reshape(1), SMEM)
    table, apart, hann = tables()
    sent = pl.pallas_call(
        split_kernel,
        out_shape=jax.ShapeDtypeStruct((BLOCKS, HOP + MEANS, width), jnp.bfloat16),
        in_specs=[HBM],
        out_specs=HBM,
        scratch_shapes=[
            pltpu.VMEM((BLOCKS, HOP, width), jnp.float32),
            pltpu.VMEM((BLOCKS, HOP + MEANS, width), jnp.bfloat16),
            pltpu.SemaphoreType.DMA((BLOCKS,)),
            pltpu.SemaphoreType.DMA((BLOCKS,)),
        ],
        compiler_params=pltpu.CompilerParams(vmem_limit_bytes=60 * 1024 * 1024),
    )(pressure)
    got = lax.all_to_all(sent, "blk", 0, 0, tiled=True)

    group = ("blk", "x", "core")
    count = float(points * lax.axis_size(SPACE))
    windowed, sums = call(
        functools.partial(sums_kernel, count),
        [
            jax.ShapeDtypeStruct((BLOCKS, BLEN, width), jnp.bfloat16),
            jax.ShapeDtypeStruct((lax.axis_size(group), 1, SUMS * freqs), jnp.float32),
        ],
        [here, got, final_steps, weights.reshape(1, points), apart, hann],
        [pltpu.VMEM((BLOCKS, 2 * HOP, width), jnp.float32), pltpu.VMEM((SUMS * HOP, 128), jnp.float32)],
    )
    sums = lax.all_to_all(sums, group, 0, 0, tiled=True)
    piece = jax.ShapeDtypeStruct((BLOCKS, 2 * freqs, width), jnp.bfloat16)
    pieces = call(
        spectra_kernel, [piece] * BLOCKS, [here, windowed, table], [pltpu.VMEM((2 * HOP, BLEN), jnp.bfloat16)]
    )
    moved = [
        lax.ppermute(value, "blk", [(i, (i + step) % BLOCKS) for i in range(BLOCKS)]) if step else value
        for step, value in enumerate(pieces)
    ]
    repeated = jax.ShapeDtypeStruct((lax.axis_size("z"), 1, SUMS * freqs), jnp.float32)
    sums = lax.all_to_all(call(repeat_kernel, repeated, [sums], cost=WAIT), "z", 0, 0, tiled=True)
    spectra = call(
        join_kernel, jax.ShapeDtypeStruct((BLOCKS, 2 * freqs, points), jnp.bfloat16), [here, *moved]
    ).reshape(BLOCKS, freqs, 2, points)
    csd = call(
        matrix_kernel, jax.ShapeDtypeStruct((2 * BLOCKS, BLOCKS, freqs), jnp.float32), [sums, (spectra, HBM)]
    )
    csd = csd.reshape(2, BLOCKS, BLOCKS, freqs)
    return (spectra, jnp.transpose(csd, (0, 3, 1, 2)))


def solution(mesh):
    across = min(4, mesh.shape["space"] // 2)
    split = Mesh(mesh.devices.reshape(-1, across, 2, mesh.shape["blk"]), (*SPACE, "blk"))
    return jax.shard_map(
        local,
        mesh=split,
        in_specs=(P("blk", SPACE), P(None, SPACE), P(SPACE)),
        out_specs=(P(None, "blk", None, SPACE), P(None, "blk", None, None)),
        check_vma=False,
    )
```

```python
import functools
import math

import jax
import jax.numpy as jnp
import numpy as np
from jax import lax
from jax.experimental import pallas as pl
from jax.experimental.pallas import tpu as pltpu
from jax.sharding import Mesh
from jax.sharding import PartitionSpec as P

HOP = 128
BLEN = 2 * HOP
BLOCKS = 4
SPACE = ("z", "x", "core")
LIMIT = 16 * 1024 * 1024
WAIT = pl.CostEstimate(flops=10**10, bytes_accessed=10**10, transcendentals=0)
MEANS = 16
PAIRS = [(i, j) for i in range(BLOCKS) for j in range(i, BLOCKS)]
CROSS = [(i, j) for i, j in PAIRS if i < j]
SUMS = len(PAIRS) + len(CROSS)

VMEM = pl.BlockSpec(memory_space=pltpu.VMEM)
SMEM = pl.BlockSpec(memory_space=pltpu.SMEM)
HBM = pl.BlockSpec(memory_space=pltpu.HBM)
ANY = pl.BlockSpec(memory_space=pl.ANY)


def tables():
    t = np.arange(BLEN)
    k = np.arange(HOP)
    angle = 2.0 * math.pi / BLEN * (k[:, None] * t[None, :] % BLEN)
    scale = 1.0 / math.sqrt(3.0 * BLEN / 8.0)
    parts = np.stack([np.cos(angle) * scale, -np.sin(angle) * scale], axis=1)
    hann = 0.5 - 0.5 * np.cos(2.0 * math.pi / BLEN * t)
    return (
        jnp.asarray(parts.reshape(2 * HOP, BLEN), jnp.bfloat16),
        jnp.asarray(parts.swapaxes(0, 1).reshape(2 * HOP, BLEN), jnp.bfloat16),
        jnp.asarray(np.repeat(hann[:, None], 128, axis=1), jnp.float32),
    )


def split_kernel(pressure_ref, out_ref, held, ready, sem_in, sem_out):
    width = out_ref.shape[2]

    def fetch(quarter):
        cols = slice(quarter * width, (quarter + 1) * width)
        return pltpu.make_async_copy(pressure_ref.at[:, cols], held.at[quarter], sem_in.at[quarter])

    def store(quarter):
        return pltpu.make_async_copy(ready.at[quarter], out_ref.at[quarter], sem_out.at[quarter])

    for quarter in range(BLOCKS):
        fetch(quarter).start()
    for quarter in range(BLOCKS):
        fetch(quarter).wait()
        x = held[quarter]
        mean = jnp.sum(x, axis=0, keepdims=True) * (1.0 / HOP)
        ready[quarter, :HOP] = (x - mean).astype(jnp.bfloat16)
        high = mean.astype(jnp.bfloat16).astype(jnp.float32)
        middle = (mean - high).astype(jnp.bfloat16).astype(jnp.float32)
        low = mean - high - middle
        row = lax.broadcasted_iota(jnp.int32, (MEANS, width), 0)
        rows = jnp.where(row == 0, high, jnp.where(row == 1, middle, jnp.where(row == 2, low, 0.0)))
        ready[quarter, HOP:] = rows.astype(jnp.bfloat16)
        store(quarter).start()
    for quarter in range(BLOCKS):
        store(quarter).wait()


def windows(segments, final, hann_ref):
    means = [jnp.sum(ref[HOP:].astype(jnp.float32), axis=0, keepdims=True) for ref in segments]
    total = jnp.sum(final, axis=0, keepdims=True) + HOP * (means[0] + means[1] + means[2] + means[3])
    mean = total / (HOP * (BLOCKS + 1))
    hann = jnp.concatenate([hann_ref[...]] * (final.shape[1] // 128), axis=1)

    def segment(s):
        if s == BLOCKS:
            return final - mean
        return segments[s][:HOP].astype(jnp.float32) + (means[s] - mean)

    blocks = []
    for b in range(BLOCKS):
        windowed = jnp.concatenate([segment(b) * hann[:HOP], segment(b + 1) * hann[HOP:]], axis=0)
        blocks.append(windowed.astype(jnp.bfloat16))
    return blocks


def sums_kernel(
    count, pos_ref, got_ref, final_ref, weights_ref, table_ref, hann_ref, out_ref, coeff, sums, rows
):
    me = pos_ref[0]
    width = got_ref.shape[2]
    own = pl.ds(pl.multiple_of(me * width, width), width)
    segments = [got_ref.at[s] for s in range(BLOCKS)]
    for b, windowed in enumerate(windows(segments, final_ref[:, own], hann_ref)):
        apart = jnp.dot(table_ref[...], windowed, preferred_element_type=jnp.float32)
        coeff[b] = apart.astype(jnp.bfloat16).astype(jnp.float32)

    weights = weights_ref[:, own] * (1.0 / count)
    freqs = HOP // BLOCKS

    def tile(t, carry):
        at = pl.multiple_of(t * 8, 8)
        acc = [None] * SUMS
        for lane in range(0, width, 128):
            cols = slice(lane, lane + 128)
            w = weights[:, cols]
            re = [coeff[b, pl.ds(at, 8), cols] for b in range(BLOCKS)]
            im = [coeff[b, pl.ds(at + HOP, 8), cols] for b in range(BLOCKS)]
            re_w = [v * w for v in re]
            im_w = [v * w for v in im]
            terms = [re_w[i] * re[j] + im_w[i] * im[j] for i, j in PAIRS]
            terms += [im_w[i] * re[j] - re_w[i] * im[j] for i, j in CROSS]
            acc = [v if a is None else a + v for a, v in zip(acc, terms)]
        first = (t // (freqs // 8)) * (SUMS * freqs) + lax.rem(t, freqs // 8) * 8
        for p in range(SUMS):
            sums[pl.ds(pl.multiple_of(first + p * freqs, 8), 8), :] = acc[p]
        return carry

    lax.fori_loop(0, HOP // 8, tile, 0)
    values = sums[...]
    high = values.astype(jnp.bfloat16)
    low = (values - high.astype(jnp.float32)).astype(jnp.bfloat16)
    ones = jnp.ones((8, 128), jnp.bfloat16)
    along = (((1,), (1,)), ((), ()))
    lanes = lax.dot_general(ones, high, along, preferred_element_type=jnp.float32)
    lanes += lax.dot_general(ones, low, along, preferred_element_type=jnp.float32)
    for row in range(rows.shape[0]):
        rows[row : row + 1] = lanes[:1, row * 128 : (row + 1) * 128]
    value = rows[...].astype(jnp.bfloat16)
    for copy in range(out_ref.shape[0]):
        out_ref[copy] = value


def fan_kernel(pos_ref, sent_ref, out1, out2, out3, sems):
    me = pos_ref[0]
    copies = []
    for step, out in enumerate((out1, out2, out3), 1):
        for place in range(BLOCKS - 1):
            quarter = lax.rem(me + step + 1 + place, BLOCKS)
            sem = sems.at[step - 1, place]
            copies.append(pltpu.make_async_copy(sent_ref.at[quarter], out.at[place], sem))
    for copy in copies:
        copy.start()
    for copy in copies:
        copy.wait()


def spectra_kernel(
    pos_ref, final_ref, table_ref, hann_ref, sent_ref, got_ref, got1, got2, got3, out_ref, held, last, ready, sems, last_sems, out_sems
):
    me = pos_ref[0]
    width = sent_ref.shape[2]
    own = BLOCKS - 1

    def cols(place):
        return pl.ds(pl.multiple_of(lax.rem(me + 1 + place, BLOCKS) * width, width), width)

    fetches = []
    for place in range(BLOCKS):
        copies = [pltpu.make_async_copy(final_ref.at[:, cols(place)], last.at[place], last_sems.at[place])]
        if place == own:
            copies.append(pltpu.make_async_copy(got_ref, held.at[place], sems.at[place, 0]))
        else:
            mine = sent_ref.at[lax.rem(me + 1 + place, BLOCKS)]
            copies.append(pltpu.make_async_copy(mine, held.at[place, me], sems.at[place, 0]))
            for step, got in enumerate((got1, got2, got3), 1):
                source = lax.rem(me + BLOCKS - step, BLOCKS)
                copies.append(
                    pltpu.make_async_copy(got.at[place], held.at[place, source], sems.at[place, step])
                )
        fetches.append(copies)
    stores = [
        pltpu.make_async_copy(ready.at[place], out_ref.at[:, :, cols(place)], out_sems.at[place])
        for place in range(BLOCKS)
    ]
    order = [own, *range(own)]
    for place in order:
        for copy in fetches[place]:
            copy.start()
    group = 2 * HOP // BLOCKS
    table = table_ref[pl.ds(pl.multiple_of(me * group, group), group), :]
    for place in order:
        for copy in fetches[place]:
            copy.wait()
        blocks = windows([held.at[place, s] for s in range(BLOCKS)], last[place], hann_ref)
        for b, windowed in enumerate(blocks):
            mixed = jnp.dot(table, windowed, preferred_element_type=jnp.float32)
            ready[place, b] = mixed.astype(jnp.bfloat16)
        stores[place].start()
    for place in order:
        stores[place].wait()


def share_kernel(got_ref, out_ref):
    total = jnp.sum(got_ref[...].astype(jnp.float32), axis=0)
    part = total.shape[0] // BLOCKS
    copies = out_ref.shape[0] // BLOCKS
    for q in range(BLOCKS):
        for copy in range(copies):
            out_ref[q * copies + copy] = total[q * part : (q + 1) * part]


def matrix_kernel(got_ref, spectra_ref, csd_ref):
    freqs = csd_ref.shape[2]
    total = jnp.sum(got_ref[...], axis=0)
    each = 128 // freqs
    rows = [total[p // each : p // each + 1, p % each * freqs : (p % each + 1) * freqs] for p in range(SUMS)]
    for i in range(BLOCKS):
        for j in range(BLOCKS):
            pair = (min(i, j), max(i, j))
            csd_ref[i, j : j + 1] = rows[PAIRS.index(pair)]
            if i == j:
                csd_ref[BLOCKS + i, j : j + 1] = jnp.zeros_like(rows[0])
            else:
                cross = rows[len(PAIRS) + CROSS.index(pair)]
                csd_ref[BLOCKS + i, j : j + 1] = cross if i < j else -cross


def call(kernel, out, operands, scratch=(), cost=None, out_spec=VMEM, limit=LIMIT):
    specs = [o[1] if isinstance(o, tuple) else VMEM for o in operands]
    return pl.pallas_call(
        kernel,
        out_shape=out,
        in_specs=specs,
        out_specs=jax.tree.map(lambda _: out_spec, out),
        scratch_shapes=scratch,
        compiler_params=pltpu.CompilerParams(vmem_limit_bytes=limit),
        cost_estimate=cost,
    )(*[o[0] if isinstance(o, tuple) else o for o in operands])


def late_first(size):
    return [(i + size // 2 + 1) % size for i in range(size)]


def local(pressure, final_steps, weights):
    points = pressure.shape[1]
    width = points // BLOCKS
    freqs = HOP // BLOCKS
    here = (lax.axis_index("blk").astype(jnp.int32).reshape(1), SMEM)
    table, apart, hann = tables()
    sent = pl.pallas_call(
        split_kernel,
        out_shape=jax.ShapeDtypeStruct((BLOCKS, HOP + MEANS, width), jnp.bfloat16),
        in_specs=[HBM],
        out_specs=HBM,
        scratch_shapes=[
            pltpu.VMEM((BLOCKS, HOP, width), jnp.float32),
            pltpu.VMEM((BLOCKS, HOP + MEANS, width), jnp.bfloat16),
            pltpu.SemaphoreType.DMA((BLOCKS,)),
            pltpu.SemaphoreType.DMA((BLOCKS,)),
        ],
        compiler_params=pltpu.CompilerParams(vmem_limit_bytes=60 * 1024 * 1024),
    )(pressure)
    got = lax.all_to_all(sent, "blk", 0, 0, tiled=True)
    part = jax.ShapeDtypeStruct((BLOCKS - 1, HOP + MEANS, width), jnp.bfloat16)
    parts = call(
        fan_kernel, [part] * 3, [here, (sent, ANY)], [pltpu.SemaphoreType.DMA((3, BLOCKS - 1))], out_spec=HBM
    )
    moved = [
        lax.ppermute(value, "blk", [(i, (i + step) % BLOCKS) for i in range(BLOCKS)])
        for step, value in enumerate(parts, 1)
    ]

    group = ("blk", "x", "core")
    count = float(points * lax.axis_size(SPACE))
    lines = SUMS * HOP // 128
    sums = call(
        functools.partial(sums_kernel, count),
        jax.ShapeDtypeStruct((lax.axis_size("z"), lines, 128), jnp.bfloat16),
        [here, got, final_steps, weights.reshape(1, points), apart, hann],
        [
            pltpu.VMEM((BLOCKS, 2 * HOP, width), jnp.float32),
            pltpu.VMEM((SUMS * HOP, 128), jnp.float32),
            pltpu.VMEM((lines, 128), jnp.float32),
        ],
        cost=WAIT,
    )
    sums = lax.all_to_all(sums, "z", 0, 0, tiled=True, axis_index_groups=[late_first(lax.axis_size("z"))])
    spectra = call(
        spectra_kernel,
        jax.ShapeDtypeStruct((BLOCKS, 2 * freqs, points), jnp.bfloat16),
        [here, (final_steps, ANY), table, hann, (sent, ANY), (got, ANY), *((value, ANY) for value in moved)],
        [
            pltpu.VMEM((BLOCKS, BLOCKS, HOP + MEANS, width), jnp.bfloat16),
            pltpu.VMEM((BLOCKS, HOP, width), jnp.float32),
            pltpu.VMEM((BLOCKS, BLOCKS, 2 * freqs, width), jnp.bfloat16),
            pltpu.SemaphoreType.DMA((BLOCKS, BLOCKS)),
            pltpu.SemaphoreType.DMA((BLOCKS,)),
            pltpu.SemaphoreType.DMA((BLOCKS,)),
        ],
        out_spec=ANY,
        limit=60 * 1024 * 1024,
    ).reshape(BLOCKS, freqs, 2, points)
    shares = jax.ShapeDtypeStruct((lax.axis_size(group), lines // BLOCKS, 128), jnp.float32)
    sums = lax.all_to_all(call(share_kernel, shares, [sums]), group, 0, 0, tiled=True)
    csd = call(matrix_kernel, jax.ShapeDtypeStruct((2 * BLOCKS, BLOCKS, freqs), jnp.float32), [sums, (spectra, ANY)])
    csd = csd.reshape(2, BLOCKS, BLOCKS, freqs)
    return (spectra, jnp.transpose(csd, (0, 3, 1, 2)))


def solution(mesh):
    across = min(4, mesh.shape["space"] // 2)
    split = Mesh(mesh.devices.reshape(-1, across, 2, mesh.shape["blk"]), (*SPACE, "blk"))
    return jax.shard_map(
        local,
        mesh=split,
        in_specs=(P("blk", SPACE), P(None, SPACE), P(SPACE)),
        out_specs=(P(None, "blk", None, SPACE), P(None, "blk", None, None)),
        check_vma=False,
    )
```

```python
import functools
import math

import jax
import jax.numpy as jnp
import numpy as np
from jax import lax
from jax.experimental import pallas as pl
from jax.experimental.pallas import tpu as pltpu
from jax.sharding import Mesh
from jax.sharding import PartitionSpec as P

HOP = 128
BLEN = 2 * HOP
BLOCKS = 4
SPACE = ("z", "x", "core")
LIMIT = 16 * 1024 * 1024
WAIT = pl.CostEstimate(flops=10**10, bytes_accessed=10**10, transcendentals=0)
MEANS = 16
PAIRS = [(i, j) for i in range(BLOCKS) for j in range(i, BLOCKS)]
CROSS = [(i, j) for i, j in PAIRS if i < j]
SUMS = len(PAIRS) + len(CROSS)

VMEM = pl.BlockSpec(memory_space=pltpu.VMEM)
SMEM = pl.BlockSpec(memory_space=pltpu.SMEM)
HBM = pl.BlockSpec(memory_space=pltpu.HBM)
ANY = pl.BlockSpec(memory_space=pl.ANY)


def tables():
    t = np.arange(BLEN)
    k = np.arange(HOP)
    angle = 2.0 * math.pi / BLEN * (k[:, None] * t[None, :] % BLEN)
    scale = 1.0 / math.sqrt(3.0 * BLEN / 8.0)
    parts = np.stack([np.cos(angle) * scale, -np.sin(angle) * scale], axis=1)
    hann = 0.5 - 0.5 * np.cos(2.0 * math.pi / BLEN * t)
    return (
        jnp.asarray(parts.reshape(2 * HOP, BLEN), jnp.bfloat16),
        jnp.asarray(parts.swapaxes(0, 1).reshape(2 * HOP, BLEN), jnp.bfloat16),
        jnp.asarray(np.repeat(hann[:, None], 128, axis=1), jnp.float32),
    )


def split_kernel(pressure_ref, out_ref, held, ready, sem_in, sem_out):
    width = out_ref.shape[2]

    def fetch(quarter):
        cols = slice(quarter * width, (quarter + 1) * width)
        return pltpu.make_async_copy(pressure_ref.at[:, cols], held.at[quarter], sem_in.at[quarter])

    def store(quarter):
        return pltpu.make_async_copy(ready.at[quarter], out_ref.at[quarter], sem_out.at[quarter])

    for quarter in range(BLOCKS):
        fetch(quarter).start()
    for quarter in range(BLOCKS):
        fetch(quarter).wait()
        x = held[quarter]
        mean = jnp.sum(x, axis=0, keepdims=True) * (1.0 / HOP)
        ready[quarter, :HOP] = (x - mean).astype(jnp.bfloat16)
        high = mean.astype(jnp.bfloat16).astype(jnp.float32)
        middle = (mean - high).astype(jnp.bfloat16).astype(jnp.float32)
        low = mean - high - middle
        row = lax.broadcasted_iota(jnp.int32, (MEANS, width), 0)
        rows = jnp.where(row == 0, high, jnp.where(row == 1, middle, jnp.where(row == 2, low, 0.0)))
        ready[quarter, HOP:] = rows.astype(jnp.bfloat16)
        store(quarter).start()
    for quarter in range(BLOCKS):
        store(quarter).wait()


def windows(segments, final, hann_ref):
    means = [jnp.sum(ref[HOP:].astype(jnp.float32), axis=0, keepdims=True) for ref in segments]
    total = jnp.sum(final, axis=0, keepdims=True) + HOP * (means[0] + means[1] + means[2] + means[3])
    mean = total / (HOP * (BLOCKS + 1))
    hann = jnp.concatenate([hann_ref[...]] * (final.shape[1] // 128), axis=1)

    def segment(s):
        if s == BLOCKS:
            return final - mean
        return segments[s][:HOP].astype(jnp.float32) + (means[s] - mean)

    blocks = []
    for b in range(BLOCKS):
        windowed = jnp.concatenate([segment(b) * hann[:HOP], segment(b + 1) * hann[HOP:]], axis=0)
        blocks.append(windowed.astype(jnp.bfloat16))
    return blocks


def sums_kernel(
    count, pos_ref, got_ref, final_ref, weights_ref, table_ref, hann_ref, out_ref, coeff, sums, rows
):
    me = pos_ref[0]
    width = got_ref.shape[2]
    own = pl.ds(pl.multiple_of(me * width, width), width)
    segments = [got_ref.at[s] for s in range(BLOCKS)]
    for b, windowed in enumerate(windows(segments, final_ref[:, own], hann_ref)):
        apart = jnp.dot(table_ref[...], windowed, preferred_element_type=jnp.float32)
        coeff[b] = apart.astype(jnp.bfloat16).astype(jnp.float32)

    weights = weights_ref[:, own] * (1.0 / count)
    freqs = HOP // BLOCKS

    def tile(t, carry):
        at = pl.multiple_of(t * 8, 8)
        acc = [None] * SUMS
        for lane in range(0, width, 128):
            cols = slice(lane, lane + 128)
            w = weights[:, cols]
            re = [coeff[b, pl.ds(at, 8), cols] for b in range(BLOCKS)]
            im = [coeff[b, pl.ds(at + HOP, 8), cols] for b in range(BLOCKS)]
            re_w = [v * w for v in re]
            im_w = [v * w for v in im]
            terms = [re_w[i] * re[j] + im_w[i] * im[j] for i, j in PAIRS]
            terms += [im_w[i] * re[j] - re_w[i] * im[j] for i, j in CROSS]
            acc = [v if a is None else a + v for a, v in zip(acc, terms)]
        first = (t // (freqs // 8)) * (SUMS * freqs) + lax.rem(t, freqs // 8) * 8
        for p in range(SUMS):
            sums[pl.ds(pl.multiple_of(first + p * freqs, 8), 8), :] = acc[p]
        return carry

    lax.fori_loop(0, HOP // 8, tile, 0)
    values = sums[...]
    high = values.astype(jnp.bfloat16)
    low = (values - high.astype(jnp.float32)).astype(jnp.bfloat16)
    ones = jnp.ones((8, 128), jnp.bfloat16)
    along = (((1,), (1,)), ((), ()))
    lanes = lax.dot_general(ones, high, along, preferred_element_type=jnp.float32)
    lanes += lax.dot_general(ones, low, along, preferred_element_type=jnp.float32)
    for row in range(rows.shape[0]):
        rows[row : row + 1] = lanes[:1, row * 128 : (row + 1) * 128]
    value = rows[...].astype(jnp.bfloat16)
    for copy in range(out_ref.shape[0]):
        out_ref[copy] = value


def fan_kernel(pos_ref, sent_ref, out1, out2, out3, sems):
    me = pos_ref[0]
    copies = []
    for step, out in enumerate((out1, out2, out3), 1):
        for place in range(BLOCKS - 1):
            quarter = lax.rem(me + step + 1 + place, BLOCKS)
            sem = sems.at[step - 1, place]
            copies.append(pltpu.make_async_copy(sent_ref.at[quarter], out.at[place], sem))
    for copy in copies:
        copy.start()
    for copy in copies:
        copy.wait()


def spectra_kernel(
    pos_ref, after_ref, final_ref, table_ref, hann_ref, sent_ref, got_ref, got1, got2, got3, out_ref, token_ref, held, last, ready, sems, last_sems, out_sems
):
    me = pos_ref[0]
    width = sent_ref.shape[2]
    own = BLOCKS - 1

    def cols(place):
        return pl.ds(pl.multiple_of(lax.rem(me + 1 + place, BLOCKS) * width, width), width)

    fetches = []
    for place in range(BLOCKS):
        copies = [pltpu.make_async_copy(final_ref.at[:, cols(place)], last.at[place], last_sems.at[place])]
        if place == own:
            copies.append(pltpu.make_async_copy(got_ref, held.at[place], sems.at[place, 0]))
        else:
            mine = sent_ref.at[lax.rem(me + 1 + place, BLOCKS)]
            copies.append(pltpu.make_async_copy(mine, held.at[place, me], sems.at[place, 0]))
            for step, got in enumerate((got1, got2, got3), 1):
                source = lax.rem(me + BLOCKS - step, BLOCKS)
                copies.append(
                    pltpu.make_async_copy(got.at[place], held.at[place, source], sems.at[place, step])
                )
        fetches.append(copies)
    stores = [
        pltpu.make_async_copy(ready.at[place], out_ref.at[:, :, :, cols(place)], out_sems.at[place])
        for place in range(BLOCKS)
    ]
    order = [own, *range(own)]
    for place in order:
        for copy in fetches[place]:
            copy.start()
    group = 2 * HOP // BLOCKS
    table = table_ref[pl.ds(pl.multiple_of(me * group, group), group), :]
    for place in order:
        for copy in fetches[place]:
            copy.wait()
        blocks = windows([held.at[place, s] for s in range(BLOCKS)], last[place], hann_ref)
        for b, windowed in enumerate(blocks):
            mixed = jnp.dot(table, windowed, preferred_element_type=jnp.float32)
            ready[place, b] = mixed.astype(jnp.bfloat16).reshape(ready.shape[2:])
        stores[place].start()
    token_ref[...] = jnp.zeros_like(token_ref)
    for place in order:
        stores[place].wait()


def token_kernel(first_ref, second_ref, token_ref):
    token_ref[...] = jnp.zeros_like(token_ref)


def share_kernel(got_ref, out_ref):
    total = jnp.sum(got_ref[...].astype(jnp.float32), axis=0)
    part = total.shape[0] // BLOCKS
    copies = out_ref.shape[0] // BLOCKS
    for q in range(BLOCKS):
        for copy in range(copies):
            out_ref[q * copies + copy] = total[q * part : (q + 1) * part]


def matrix_kernel(got_ref, csd_ref):
    freqs = csd_ref.shape[2]
    total = jnp.sum(got_ref[...], axis=0)
    each = 128 // freqs
    rows = [total[p // each : p // each + 1, p % each * freqs : (p % each + 1) * freqs] for p in range(SUMS)]
    for i in range(BLOCKS):
        for j in range(BLOCKS):
            pair = (min(i, j), max(i, j))
            csd_ref[i, j : j + 1] = rows[PAIRS.index(pair)]
            if i == j:
                csd_ref[BLOCKS + i, j : j + 1] = jnp.zeros_like(rows[0])
            else:
                cross = rows[len(PAIRS) + CROSS.index(pair)]
                csd_ref[BLOCKS + i, j : j + 1] = cross if i < j else -cross


def call(kernel, out, operands, scratch=(), cost=None, out_spec=VMEM, limit=LIMIT):
    specs = [o[1] if isinstance(o, tuple) else VMEM for o in operands]
    return pl.pallas_call(
        kernel,
        out_shape=out,
        in_specs=specs,
        out_specs=out_spec,
        scratch_shapes=scratch,
        compiler_params=pltpu.CompilerParams(vmem_limit_bytes=limit),
        cost_estimate=cost,
    )(*[o[0] if isinstance(o, tuple) else o for o in operands])


def late_first(size):
    return [(i + size // 2 + 1) % size for i in range(size)]


def local(pressure, final_steps, weights):
    points = pressure.shape[1]
    width = points // BLOCKS
    freqs = HOP // BLOCKS
    here = (lax.axis_index("blk").astype(jnp.int32).reshape(1), SMEM)
    table, apart, hann = tables()
    sent = pl.pallas_call(
        split_kernel,
        out_shape=jax.ShapeDtypeStruct((BLOCKS, HOP + MEANS, width), jnp.bfloat16),
        in_specs=[HBM],
        out_specs=HBM,
        scratch_shapes=[
            pltpu.VMEM((BLOCKS, HOP, width), jnp.float32),
            pltpu.VMEM((BLOCKS, HOP + MEANS, width), jnp.bfloat16),
            pltpu.SemaphoreType.DMA((BLOCKS,)),
            pltpu.SemaphoreType.DMA((BLOCKS,)),
        ],
        compiler_params=pltpu.CompilerParams(vmem_limit_bytes=60 * 1024 * 1024),
    )(pressure)
    got = lax.all_to_all(sent, "blk", 0, 0, tiled=True)
    part = jax.ShapeDtypeStruct((BLOCKS - 1, HOP + MEANS, width), jnp.bfloat16)
    parts = call(
        fan_kernel, [part] * 3, [here, (sent, ANY)], [pltpu.SemaphoreType.DMA((3, BLOCKS - 1))], out_spec=[HBM] * 3
    )
    moved = [
        lax.ppermute(value, "blk", [(i, (i + step) % BLOCKS) for i in range(BLOCKS)])
        for step, value in enumerate(parts, 1)
    ]

    group = ("blk", "x", "core")
    count = float(points * lax.axis_size(SPACE))
    lines = SUMS * HOP // 128
    sums = call(
        functools.partial(sums_kernel, count),
        jax.ShapeDtypeStruct((lax.axis_size("z"), lines, 128), jnp.bfloat16),
        [here, got, final_steps, weights.reshape(1, points), apart, hann],
        [
            pltpu.VMEM((BLOCKS, 2 * HOP, width), jnp.float32),
            pltpu.VMEM((SUMS * HOP, 128), jnp.float32),
            pltpu.VMEM((lines, 128), jnp.float32),
        ],
        cost=WAIT,
    )
    sums = lax.all_to_all(sums, "z", 0, 0, tiled=True, axis_index_groups=[late_first(lax.axis_size("z"))])
    token = jax.ShapeDtypeStruct((8, 128), jnp.float32)
    after = call(
        token_kernel, token, [(moved[0], ANY), (moved[1], ANY)], cost=WAIT, limit=60 * 1024 * 1024
    )
    spectra, token = call(
        spectra_kernel,
        [jax.ShapeDtypeStruct((BLOCKS, freqs, 2, points), jnp.bfloat16), token],
        [here, after, (final_steps, ANY), table, hann, (sent, ANY), (got, ANY), *((value, ANY) for value in moved)],
        [
            pltpu.VMEM((BLOCKS, BLOCKS, HOP + MEANS, width), jnp.bfloat16),
            pltpu.VMEM((BLOCKS, HOP, width), jnp.float32),
            pltpu.VMEM((BLOCKS, BLOCKS, freqs, 2, width), jnp.bfloat16),
            pltpu.SemaphoreType.DMA((BLOCKS, BLOCKS)),
            pltpu.SemaphoreType.DMA((BLOCKS,)),
            pltpu.SemaphoreType.DMA((BLOCKS,)),
        ],
        out_spec=[ANY, VMEM],
        limit=60 * 1024 * 1024,
    )
    shares = jax.ShapeDtypeStruct((lax.axis_size(group), lines // BLOCKS, 128), jnp.float32)
    sums = lax.all_to_all(call(share_kernel, shares, [sums]), group, 0, 0, tiled=True)
    csd = call(matrix_kernel, jax.ShapeDtypeStruct((2 * BLOCKS, BLOCKS, freqs), jnp.float32), [sums])
    csd = csd.reshape(2, BLOCKS, BLOCKS, freqs)
    return (spectra, jnp.transpose(csd, (0, 3, 1, 2)))


def solution(mesh):
    across = min(4, mesh.shape["space"] // 2)
    split = Mesh(mesh.devices.reshape(-1, across, 2, mesh.shape["blk"]), (*SPACE, "blk"))
    return jax.shard_map(
        local,
        mesh=split,
        in_specs=(P("blk", SPACE), P(None, SPACE), P(SPACE)),
        out_specs=(P(None, "blk", None, SPACE), P(None, "blk", None, None)),
        check_vma=False,
    )
```

```python
import functools
import math

import jax
import jax.numpy as jnp
import numpy as np
from jax import lax
from jax.experimental import pallas as pl
from jax.experimental.pallas import tpu as pltpu
from jax.sharding import Mesh
from jax.sharding import PartitionSpec as P

HOP = 128
BLEN = 2 * HOP
BLOCKS = 4
SPACE = ("z", "x", "core")
LIMIT = 16 * 1024 * 1024
WAIT = pl.CostEstimate(flops=10**10, bytes_accessed=10**10, transcendentals=0)
MEANS = 16
PAIRS = [(i, j) for i in range(BLOCKS) for j in range(i, BLOCKS)]
CROSS = [(i, j) for i, j in PAIRS if i < j]
SUMS = len(PAIRS) + len(CROSS)

VMEM = pl.BlockSpec(memory_space=pltpu.VMEM)
SMEM = pl.BlockSpec(memory_space=pltpu.SMEM)
HBM = pl.BlockSpec(memory_space=pltpu.HBM)
ANY = pl.BlockSpec(memory_space=pl.ANY)


def tables():
    t = np.arange(BLEN)
    k = np.arange(HOP)
    angle = 2.0 * math.pi / BLEN * (k[:, None] * t[None, :] % BLEN)
    scale = 1.0 / math.sqrt(3.0 * BLEN / 8.0)
    parts = np.stack([np.cos(angle) * scale, -np.sin(angle) * scale], axis=1)
    return (
        jnp.asarray(parts.reshape(2 * HOP, BLEN), jnp.bfloat16),
        jnp.asarray(parts.swapaxes(0, 1).reshape(2 * HOP, BLEN), jnp.bfloat16),
    )


def split_kernel(pressure_ref, out_ref, held, ready, sem_in, sem_out):
    width = out_ref.shape[2]

    def fetch(quarter):
        cols = slice(quarter * width, (quarter + 1) * width)
        return pltpu.make_async_copy(pressure_ref.at[:, cols], held.at[quarter], sem_in.at[quarter])

    def store(quarter):
        return pltpu.make_async_copy(ready.at[quarter], out_ref.at[quarter], sem_out.at[quarter])

    for quarter in range(BLOCKS):
        fetch(quarter).start()
    for quarter in range(BLOCKS):
        fetch(quarter).wait()
        x = held[quarter]
        mean = jnp.sum(x, axis=0, keepdims=True) * (1.0 / HOP)
        ready[quarter, :HOP] = (x - mean).astype(jnp.bfloat16)
        high = mean.astype(jnp.bfloat16).astype(jnp.float32)
        middle = (mean - high).astype(jnp.bfloat16).astype(jnp.float32)
        low = mean - high - middle
        row = lax.broadcasted_iota(jnp.int32, (MEANS, width), 0)
        rows = jnp.where(row == 0, high, jnp.where(row == 1, middle, jnp.where(row == 2, low, 0.0)))
        ready[quarter, HOP:] = rows.astype(jnp.bfloat16)
        store(quarter).start()
    for quarter in range(BLOCKS):
        store(quarter).wait()


def window():
    t = lax.broadcasted_iota(jnp.int32, (BLEN, 128), 0).astype(jnp.float32)
    square = ((t - HOP) * (math.pi / BLEN)) ** 2
    cosine = jnp.full_like(square, 1.0 / math.factorial(12))
    for order in range(10, -1, -2):
        cosine = cosine * square + (-1.0) ** (order // 2) / math.factorial(order)
    return cosine * cosine


def windows(segments, final, hann):
    means = [jnp.sum(ref[HOP:].astype(jnp.float32), axis=0, keepdims=True) for ref in segments]
    total = jnp.sum(final, axis=0, keepdims=True) + HOP * (means[0] + means[1] + means[2] + means[3])
    mean = total / (HOP * (BLOCKS + 1))
    hann = jnp.concatenate([hann] * (final.shape[1] // 128), axis=1)

    def segment(s):
        if s == BLOCKS:
            return final - mean
        return segments[s][:HOP].astype(jnp.float32) + (means[s] - mean)

    blocks = []
    for b in range(BLOCKS):
        windowed = jnp.concatenate([segment(b) * hann[:HOP], segment(b + 1) * hann[HOP:]], axis=0)
        blocks.append(windowed.astype(jnp.bfloat16))
    return blocks


def sums_kernel(
    count, pos_ref, got_ref, final_ref, weights_ref, table_ref, out_ref, coeff, sums, rows
):
    me = pos_ref[0]
    width = got_ref.shape[2]
    own = pl.ds(pl.multiple_of(me * width, width), width)
    segments = [got_ref.at[s] for s in range(BLOCKS)]
    for b, windowed in enumerate(windows(segments, final_ref[:, own], window())):
        apart = jnp.dot(table_ref[...], windowed, preferred_element_type=jnp.float32)
        coeff[b] = apart.astype(jnp.bfloat16).astype(jnp.float32)

    weights = weights_ref[:, own] * (1.0 / count)
    freqs = HOP // BLOCKS

    def tile(t, carry):
        at = pl.multiple_of(t * 8, 8)
        acc = [None] * SUMS
        for lane in range(0, width, 128):
            cols = slice(lane, lane + 128)
            w = weights[:, cols]
            re = [coeff[b, pl.ds(at, 8), cols] for b in range(BLOCKS)]
            im = [coeff[b, pl.ds(at + HOP, 8), cols] for b in range(BLOCKS)]
            re_w = [v * w for v in re]
            im_w = [v * w for v in im]
            terms = [re_w[i] * re[j] + im_w[i] * im[j] for i, j in PAIRS]
            terms += [im_w[i] * re[j] - re_w[i] * im[j] for i, j in CROSS]
            acc = [v if a is None else a + v for a, v in zip(acc, terms)]
        first = (t // (freqs // 8)) * (SUMS * freqs) + lax.rem(t, freqs // 8) * 8
        for p in range(SUMS):
            sums[pl.ds(pl.multiple_of(first + p * freqs, 8), 8), :] = acc[p]
        return carry

    lax.fori_loop(0, HOP // 8, tile, 0)
    values = sums[...]
    high = values.astype(jnp.bfloat16)
    low = (values - high.astype(jnp.float32)).astype(jnp.bfloat16)
    ones = jnp.ones((8, 128), jnp.bfloat16)
    along = (((1,), (1,)), ((), ()))
    lanes = lax.dot_general(ones, high, along, preferred_element_type=jnp.float32)
    lanes += lax.dot_general(ones, low, along, preferred_element_type=jnp.float32)
    for row in range(rows.shape[0]):
        rows[row : row + 1] = lanes[:1, row * 128 : (row + 1) * 128]
    value = rows[...].astype(jnp.bfloat16)
    for copy in range(out_ref.shape[0]):
        out_ref[copy] = value


def fan_kernel(steps, pos_ref, sent_ref, *refs):
    *outs, sems = refs[len(refs) - len(steps) - 1 :]
    me = pos_ref[0]
    copies = []
    for at, (step, out) in enumerate(zip(steps, outs)):
        for place in range(BLOCKS - 1):
            quarter = lax.rem(me + step + 1 + place, BLOCKS)
            copies.append(pltpu.make_async_copy(sent_ref.at[quarter], out.at[place], sems.at[at, place]))
    for copy in copies:
        copy.start()
    for copy in copies:
        copy.wait()


def spectra_kernel(
    pos_ref, after_ref, final_ref, table_ref, own_ref, got_ref, got1, got2, got3, out_ref, token_ref, held, last, ready, sems, last_sems, out_sems
):
    me = pos_ref[0]
    width = own_ref.shape[2]
    own = BLOCKS - 1
    hann = window()

    def cols(place):
        return pl.ds(pl.multiple_of(lax.rem(me + 1 + place, BLOCKS) * width, width), width)

    fetches = []
    for place in range(BLOCKS):
        copies = [pltpu.make_async_copy(final_ref.at[:, cols(place)], last.at[place], last_sems.at[place])]
        if place == own:
            copies.append(pltpu.make_async_copy(got_ref, held.at[place], sems.at[place, 0]))
        else:
            mine = own_ref.at[lax.rem(me + 1 + place, BLOCKS)]
            copies.append(pltpu.make_async_copy(mine, held.at[place, me], sems.at[place, 0]))
            for step, got in enumerate((got1, got2, got3), 1):
                source = lax.rem(me + BLOCKS - step, BLOCKS)
                copies.append(
                    pltpu.make_async_copy(got.at[place], held.at[place, source], sems.at[place, step])
                )
        fetches.append(copies)
    stores = [
        pltpu.make_async_copy(ready.at[place], out_ref.at[:, :, :, cols(place)], out_sems.at[place])
        for place in range(BLOCKS)
    ]
    order = [own, *range(own)]
    for place in order:
        for copy in fetches[place]:
            copy.start()
    group = 2 * HOP // BLOCKS
    table = table_ref[pl.ds(pl.multiple_of(me * group, group), group), :]
    for place in order:
        for copy in fetches[place]:
            copy.wait()
        blocks = windows([held.at[place, s] for s in range(BLOCKS)], last[place], hann)
        for b, windowed in enumerate(blocks):
            mixed = jnp.dot(table, windowed, preferred_element_type=jnp.float32)
            ready[place, b] = mixed.astype(jnp.bfloat16).reshape(ready.shape[2:])
        stores[place].start()
    token_ref[...] = jnp.zeros_like(token_ref)
    for place in order:
        stores[place].wait()


def token_kernel(first_ref, second_ref, token_ref):
    token_ref[...] = jnp.zeros_like(token_ref)


def share_kernel(got_ref, out_ref):
    total = jnp.sum(got_ref[...].astype(jnp.float32), axis=0)
    part = total.shape[0] // BLOCKS
    copies = out_ref.shape[0] // BLOCKS
    for q in range(BLOCKS):
        for copy in range(copies):
            out_ref[q * copies + copy] = total[q * part : (q + 1) * part]


def matrix_kernel(got_ref, csd_ref):
    freqs = csd_ref.shape[2]
    total = jnp.sum(got_ref[...], axis=0)
    each = 128 // freqs
    rows = [total[p // each : p // each + 1, p % each * freqs : (p % each + 1) * freqs] for p in range(SUMS)]
    for i in range(BLOCKS):
        for j in range(BLOCKS):
            pair = (min(i, j), max(i, j))
            csd_ref[i, j : j + 1] = rows[PAIRS.index(pair)]
            if i == j:
                csd_ref[BLOCKS + i, j : j + 1] = jnp.zeros_like(rows[0])
            else:
                cross = rows[len(PAIRS) + CROSS.index(pair)]
                csd_ref[BLOCKS + i, j : j + 1] = cross if i < j else -cross


def call(kernel, out, operands, scratch=(), cost=None, out_spec=VMEM, limit=LIMIT):
    specs = [o[1] if isinstance(o, tuple) else VMEM for o in operands]
    return pl.pallas_call(
        kernel,
        out_shape=out,
        in_specs=specs,
        out_specs=out_spec,
        scratch_shapes=scratch,
        compiler_params=pltpu.CompilerParams(vmem_limit_bytes=limit),
        cost_estimate=cost,
    )(*[o[0] if isinstance(o, tuple) else o for o in operands])


def late_first(size):
    return [(i + size // 2 + 1) % size for i in range(size)]


def local(pressure, final_steps, weights):
    points = pressure.shape[1]
    width = points // BLOCKS
    freqs = HOP // BLOCKS
    here = (lax.axis_index("blk").astype(jnp.int32).reshape(1), SMEM)
    table, apart = tables()
    sent = pl.pallas_call(
        split_kernel,
        out_shape=jax.ShapeDtypeStruct((BLOCKS, HOP + MEANS, width), jnp.bfloat16),
        in_specs=[HBM],
        out_specs=HBM,
        scratch_shapes=[
            pltpu.VMEM((BLOCKS, HOP, width), jnp.float32),
            pltpu.VMEM((BLOCKS, HOP + MEANS, width), jnp.bfloat16),
            pltpu.SemaphoreType.DMA((BLOCKS,)),
            pltpu.SemaphoreType.DMA((BLOCKS,)),
        ],
        compiler_params=pltpu.CompilerParams(vmem_limit_bytes=60 * 1024 * 1024),
    )(pressure)
    got = lax.all_to_all(sent, "blk", 0, 0, tiled=True)
    part = jax.ShapeDtypeStruct((BLOCKS - 1, HOP + MEANS, width), jnp.bfloat16)

    def passed_on(steps, near):
        parts = call(
            functools.partial(fan_kernel, steps),
            [part] * len(steps),
            [here, (sent, ANY), *near],
            [pltpu.SemaphoreType.DMA((len(steps), BLOCKS - 1))],
            out_spec=[HBM] * len(steps),
        )
        return [
            lax.ppermute(value, "blk", [(i, (i + step) % BLOCKS) for i in range(BLOCKS)])
            for step, value in zip(steps, parts)
        ]

    moved = passed_on((1, 2), [apart, weights.reshape(1, points), table]) + passed_on((3,), [])

    group = ("blk", "x", "core")
    count = float(points * lax.axis_size(SPACE))
    lines = SUMS * HOP // 128
    sums = call(
        functools.partial(sums_kernel, count),
        jax.ShapeDtypeStruct((lax.axis_size("z"), lines, 128), jnp.bfloat16),
        [here, got, final_steps, weights.reshape(1, points), apart],
        [
            pltpu.VMEM((BLOCKS, 2 * HOP, width), jnp.float32),
            pltpu.VMEM((SUMS * HOP, 128), jnp.float32),
            pltpu.VMEM((lines, 128), jnp.float32),
        ],
        cost=WAIT,
    )
    sums = lax.all_to_all(sums, "z", 0, 0, tiled=True, axis_index_groups=[late_first(lax.axis_size("z"))])
    token = jax.ShapeDtypeStruct((8, 128), jnp.float32)
    after = call(
        token_kernel, token, [(moved[0], ANY), (moved[1], ANY)], cost=WAIT
    )
    spectra, token = call(
        spectra_kernel,
        [jax.ShapeDtypeStruct((BLOCKS, freqs, 2, points), jnp.bfloat16), token],
        [here, after, (final_steps, ANY), table, (sent, ANY), (got, ANY), *((value, ANY) for value in moved)],
        [
            pltpu.VMEM((BLOCKS, BLOCKS, HOP + MEANS, width), jnp.bfloat16),
            pltpu.VMEM((BLOCKS, HOP, width), jnp.float32),
            pltpu.VMEM((BLOCKS, BLOCKS, freqs, 2, width), jnp.bfloat16),
            pltpu.SemaphoreType.DMA((BLOCKS, BLOCKS)),
            pltpu.SemaphoreType.DMA((BLOCKS,)),
            pltpu.SemaphoreType.DMA((BLOCKS,)),
        ],
        out_spec=[ANY, VMEM],
    )
    shares = jax.ShapeDtypeStruct((lax.axis_size(group), lines // BLOCKS, 128), jnp.float32)
    sums = lax.all_to_all(call(share_kernel, shares, [sums]), group, 0, 0, tiled=True)
    csd = call(matrix_kernel, jax.ShapeDtypeStruct((2 * BLOCKS, BLOCKS, freqs), jnp.float32), [sums])
    csd = csd.reshape(2, BLOCKS, BLOCKS, freqs)
    return (spectra, jnp.transpose(csd, (0, 3, 1, 2)))


def solution(mesh):
    across = min(4, mesh.shape["space"] // 2)
    split = Mesh(mesh.devices.reshape(-1, across, 2, mesh.shape["blk"]), (*SPACE, "blk"))
    return jax.shard_map(
        local,
        mesh=split,
        in_specs=(P("blk", SPACE), P(None, SPACE), P(SPACE)),
        out_specs=(P(None, "blk", None, SPACE), P(None, "blk", None, None)),
        check_vma=False,
    )
```

```python
import functools
import math

import jax
import jax.numpy as jnp
import numpy as np
from jax import lax
from jax.experimental import pallas as pl
from jax.experimental.pallas import tpu as pltpu
from jax.sharding import Mesh
from jax.sharding import PartitionSpec as P

HOP = 128
BLEN = 2 * HOP
BLOCKS = 4
SPACE = ("z", "x", "core")
LIMIT = 16 * 1024 * 1024
WAIT = pl.CostEstimate(flops=10**10, bytes_accessed=10**10, transcendentals=0)
MEANS = 16
PAIRS = [(i, j) for i in range(BLOCKS) for j in range(i, BLOCKS)]
CROSS = [(i, j) for i, j in PAIRS if i < j]
SUMS = len(PAIRS) + len(CROSS)

VMEM = pl.BlockSpec(memory_space=pltpu.VMEM)
SMEM = pl.BlockSpec(memory_space=pltpu.SMEM)
HBM = pl.BlockSpec(memory_space=pltpu.HBM)
ANY = pl.BlockSpec(memory_space=pl.ANY)


def tables():
    t = np.arange(BLEN)
    k = np.arange(HOP)
    angle = 2.0 * math.pi / BLEN * (k[:, None] * t[None, :] % BLEN)
    scale = 1.0 / math.sqrt(3.0 * BLEN / 8.0)
    parts = np.stack([np.cos(angle) * scale, -np.sin(angle) * scale], axis=1)
    return (
        jnp.asarray(parts.reshape(2 * HOP, BLEN), jnp.bfloat16),
        jnp.asarray(parts.swapaxes(0, 1).reshape(2 * HOP, BLEN), jnp.bfloat16),
    )


def split_kernel(pressure_ref, out_ref, held, ready, sem_in, sem_out):
    width = out_ref.shape[2]

    def fetch(quarter):
        cols = slice(quarter * width, (quarter + 1) * width)
        return pltpu.make_async_copy(pressure_ref.at[:, cols], held.at[quarter], sem_in.at[quarter])

    def store(quarter):
        return pltpu.make_async_copy(ready.at[quarter], out_ref.at[quarter], sem_out.at[quarter])

    for quarter in range(BLOCKS):
        fetch(quarter).start()
    for quarter in range(BLOCKS):
        fetch(quarter).wait()
        x = held[quarter]
        mean = jnp.sum(x, axis=0, keepdims=True) * (1.0 / HOP)
        ready[quarter, :HOP] = (x - mean).astype(jnp.bfloat16)
        high = mean.astype(jnp.bfloat16).astype(jnp.float32)
        middle = (mean - high).astype(jnp.bfloat16).astype(jnp.float32)
        low = mean - high - middle
        row = lax.broadcasted_iota(jnp.int32, (MEANS, width), 0)
        rows = jnp.where(row == 0, high, jnp.where(row == 1, middle, jnp.where(row == 2, low, 0.0)))
        ready[quarter, HOP:] = rows.astype(jnp.bfloat16)
        store(quarter).start()
    for quarter in range(BLOCKS):
        store(quarter).wait()


def window():
    t = lax.broadcasted_iota(jnp.int32, (BLEN, 128), 0).astype(jnp.float32)
    square = ((t - HOP) * (math.pi / BLEN)) ** 2
    cosine = jnp.full_like(square, 1.0 / math.factorial(12))
    for order in range(10, -1, -2):
        cosine = cosine * square + (-1.0) ** (order // 2) / math.factorial(order)
    return cosine * cosine


def windows(segments, final, hann):
    means = [jnp.sum(ref[HOP:].astype(jnp.float32), axis=0, keepdims=True) for ref in segments]
    total = jnp.sum(final, axis=0, keepdims=True) + HOP * (means[0] + means[1] + means[2] + means[3])
    mean = total / (HOP * (BLOCKS + 1))
    hann = jnp.concatenate([hann] * (final.shape[1] // 128), axis=1)

    def segment(s):
        if s == BLOCKS:
            return final - mean
        return segments[s][:HOP].astype(jnp.float32) + (means[s] - mean)

    blocks = []
    for b in range(BLOCKS):
        windowed = jnp.concatenate([segment(b) * hann[:HOP], segment(b + 1) * hann[HOP:]], axis=0)
        blocks.append(windowed.astype(jnp.bfloat16))
    return blocks


def sums_kernel(
    count, pos_ref, got_ref, final_ref, weights_ref, table_ref, out_ref, coeff, sums, rows
):
    me = pos_ref[0]
    width = got_ref.shape[2]
    own = pl.ds(pl.multiple_of(me * width, width), width)
    segments = [got_ref.at[s] for s in range(BLOCKS)]
    for b, windowed in enumerate(windows(segments, final_ref[:, own], window())):
        apart = jnp.dot(table_ref[...], windowed, preferred_element_type=jnp.float32)
        coeff[b] = apart.astype(jnp.bfloat16).astype(jnp.float32)

    weights = weights_ref[:, own] * (1.0 / count)
    freqs = HOP // BLOCKS

    def tile(t, carry):
        at = pl.multiple_of(t * 8, 8)
        acc = [None] * SUMS
        for lane in range(0, width, 128):
            cols = slice(lane, lane + 128)
            w = weights[:, cols]
            re = [coeff[b, pl.ds(at, 8), cols] for b in range(BLOCKS)]
            im = [coeff[b, pl.ds(at + HOP, 8), cols] for b in range(BLOCKS)]
            re_w = [v * w for v in re]
            im_w = [v * w for v in im]
            terms = [re_w[i] * re[j] + im_w[i] * im[j] for i, j in PAIRS]
            terms += [im_w[i] * re[j] - re_w[i] * im[j] for i, j in CROSS]
            acc = [v if a is None else a + v for a, v in zip(acc, terms)]
        first = (t // (freqs // 8)) * (SUMS * freqs) + lax.rem(t, freqs // 8) * 8
        for p in range(SUMS):
            sums[pl.ds(pl.multiple_of(first + p * freqs, 8), 8), :] = acc[p]
        return carry

    lax.fori_loop(0, HOP // 8, tile, 0)
    ones = jnp.ones((8, 128), jnp.bfloat16)
    along = (((1,), (1,)), ((), ()))
    lanes = lax.dot_general(ones, sums[...].astype(jnp.bfloat16), along, preferred_element_type=jnp.float32)
    for row in range(rows.shape[0]):
        rows[row : row + 1] = lanes[:1, row * 128 : (row + 1) * 128]
    value = rows[...].astype(jnp.bfloat16)
    for copy in range(out_ref.shape[0]):
        out_ref[copy] = value


def fan_kernel(steps, pos_ref, sent_ref, *refs):
    *outs, sems = refs[len(refs) - len(steps) - 1 :]
    me = pos_ref[0]
    copies = []
    for at, (step, out) in enumerate(zip(steps, outs)):
        for place in range(BLOCKS - 1):
            quarter = lax.rem(me + step + 1 + place, BLOCKS)
            copies.append(pltpu.make_async_copy(sent_ref.at[quarter], out.at[place], sems.at[at, place]))
    for copy in copies:
        copy.start()
    for copy in copies:
        copy.wait()


def spectra_kernel(
    pos_ref, after_ref, final_ref, table_ref, own_ref, got_ref, got1, got2, got3, out_ref, token_ref, held, last, ready, sems, last_sems, out_sems
):
    me = pos_ref[0]
    width = own_ref.shape[2]
    own = BLOCKS - 1
    hann = window()

    def cols(place):
        return pl.ds(pl.multiple_of(lax.rem(me + 1 + place, BLOCKS) * width, width), width)

    fetches = []
    for place in range(BLOCKS):
        copies = [pltpu.make_async_copy(final_ref.at[:, cols(place)], last.at[place], last_sems.at[place])]
        if place == own:
            copies.append(pltpu.make_async_copy(got_ref, held.at[place], sems.at[place, 0]))
        else:
            mine = own_ref.at[lax.rem(me + 1 + place, BLOCKS)]
            copies.append(pltpu.make_async_copy(mine, held.at[place, me], sems.at[place, 0]))
            for step, got in enumerate((got1, got2, got3), 1):
                source = lax.rem(me + BLOCKS - step, BLOCKS)
                copies.append(
                    pltpu.make_async_copy(got.at[place], held.at[place, source], sems.at[place, step])
                )
        fetches.append(copies)
    stores = [
        pltpu.make_async_copy(ready.at[place], out_ref.at[:, :, :, cols(place)], out_sems.at[place])
        for place in range(BLOCKS)
    ]
    order = [own, *range(own)]
    for place in order:
        for copy in fetches[place]:
            copy.start()
    group = 2 * HOP // BLOCKS
    table = table_ref[pl.ds(pl.multiple_of(me * group, group), group), :]
    for place in order:
        for copy in fetches[place]:
            copy.wait()
        blocks = windows([held.at[place, s] for s in range(BLOCKS)], last[place], hann)
        for b, windowed in enumerate(blocks):
            mixed = jnp.dot(table, windowed, preferred_element_type=jnp.float32)
            ready[place, b] = mixed.astype(jnp.bfloat16).reshape(ready.shape[2:])
        stores[place].start()
    token_ref[...] = jnp.zeros_like(token_ref)
    for place in order:
        stores[place].wait()


def token_kernel(first_ref, second_ref, token_ref):
    token_ref[...] = jnp.zeros_like(token_ref)


def share_kernel(got_ref, out_ref):
    total = jnp.sum(got_ref[...].astype(jnp.float32), axis=0)
    part = total.shape[0] // BLOCKS
    copies = out_ref.shape[0] // BLOCKS
    for q in range(BLOCKS):
        for copy in range(copies):
            out_ref[q * copies + copy] = total[q * part : (q + 1) * part].astype(out_ref.dtype)


def matrix_kernel(got_ref, csd_ref):
    freqs = csd_ref.shape[2]
    total = jnp.sum(got_ref[...].astype(jnp.float32), axis=0)
    each = 128 // freqs
    rows = [total[p // each : p // each + 1, p % each * freqs : (p % each + 1) * freqs] for p in range(SUMS)]
    for i in range(BLOCKS):
        for j in range(BLOCKS):
            pair = (min(i, j), max(i, j))
            csd_ref[i, j : j + 1] = rows[PAIRS.index(pair)]
            if i == j:
                csd_ref[BLOCKS + i, j : j + 1] = jnp.zeros_like(rows[0])
            else:
                cross = rows[len(PAIRS) + CROSS.index(pair)]
                csd_ref[BLOCKS + i, j : j + 1] = cross if i < j else -cross


def call(kernel, out, operands, scratch=(), cost=None, out_spec=VMEM, limit=LIMIT):
    specs = [o[1] if isinstance(o, tuple) else VMEM for o in operands]
    return pl.pallas_call(
        kernel,
        out_shape=out,
        in_specs=specs,
        out_specs=out_spec,
        scratch_shapes=scratch,
        compiler_params=pltpu.CompilerParams(vmem_limit_bytes=limit),
        cost_estimate=cost,
    )(*[o[0] if isinstance(o, tuple) else o for o in operands])


def late_first(size):
    return [(i + size // 2 + 3) % size for i in range(size)]


def local(pressure, final_steps, weights):
    points = pressure.shape[1]
    width = points // BLOCKS
    freqs = HOP // BLOCKS
    here = (lax.axis_index("blk").astype(jnp.int32).reshape(1), SMEM)
    table, apart = tables()
    sent = pl.pallas_call(
        split_kernel,
        out_shape=jax.ShapeDtypeStruct((BLOCKS, HOP + MEANS, width), jnp.bfloat16),
        in_specs=[HBM],
        out_specs=HBM,
        scratch_shapes=[
            pltpu.VMEM((BLOCKS, HOP, width), jnp.float32),
            pltpu.VMEM((BLOCKS, HOP + MEANS, width), jnp.bfloat16),
            pltpu.SemaphoreType.DMA((BLOCKS,)),
            pltpu.SemaphoreType.DMA((BLOCKS,)),
        ],
        compiler_params=pltpu.CompilerParams(vmem_limit_bytes=60 * 1024 * 1024),
    )(pressure)
    got = lax.all_to_all(sent, "blk", 0, 0, tiled=True)
    part = jax.ShapeDtypeStruct((BLOCKS - 1, HOP + MEANS, width), jnp.bfloat16)

    def passed_on(steps, near):
        parts = call(
            functools.partial(fan_kernel, steps),
            [part] * len(steps),
            [here, (sent, ANY), *near],
            [pltpu.SemaphoreType.DMA((len(steps), BLOCKS - 1))],
            out_spec=[HBM] * len(steps),
        )
        return [
            lax.ppermute(value, "blk", [(i, (i + step) % BLOCKS) for i in range(BLOCKS)])
            for step, value in zip(steps, parts)
        ]

    moved = passed_on((1, 2), [apart, weights.reshape(1, points), table]) + passed_on((3,), [])

    group = ("blk", "x", "core")
    count = float(points * lax.axis_size(SPACE))
    lines = SUMS * HOP // 128
    sums = call(
        functools.partial(sums_kernel, count),
        jax.ShapeDtypeStruct((lax.axis_size("z"), lines, 128), jnp.bfloat16),
        [here, got, final_steps, weights.reshape(1, points), apart],
        [
            pltpu.VMEM((BLOCKS, 2 * HOP, width), jnp.float32),
            pltpu.VMEM((SUMS * HOP, 128), jnp.float32),
            pltpu.VMEM((lines, 128), jnp.float32),
        ],
        cost=WAIT,
    )
    sums = lax.all_to_all(sums, "z", 0, 0, tiled=True, axis_index_groups=[late_first(lax.axis_size("z"))])
    token = jax.ShapeDtypeStruct((8, 128), jnp.float32)
    after = call(
        token_kernel, token, [(moved[0], ANY), (moved[1], ANY)], cost=WAIT
    )
    spectra, token = call(
        spectra_kernel,
        [jax.ShapeDtypeStruct((BLOCKS, freqs, 2, points), jnp.bfloat16), token],
        [here, after, (final_steps, ANY), table, (sent, ANY), (got, ANY), *((value, ANY) for value in moved)],
        [
            pltpu.VMEM((BLOCKS, BLOCKS, HOP + MEANS, width), jnp.bfloat16),
            pltpu.VMEM((BLOCKS, HOP, width), jnp.float32),
            pltpu.VMEM((BLOCKS, BLOCKS, freqs, 2, width), jnp.bfloat16),
            pltpu.SemaphoreType.DMA((BLOCKS, BLOCKS)),
            pltpu.SemaphoreType.DMA((BLOCKS,)),
            pltpu.SemaphoreType.DMA((BLOCKS,)),
        ],
        out_spec=[ANY, VMEM],
    )
    shares = jax.ShapeDtypeStruct((lax.axis_size(group), lines // BLOCKS, 128), jnp.bfloat16)
    sums = lax.all_to_all(call(share_kernel, shares, [sums]), group, 0, 0, tiled=True)
    csd = call(matrix_kernel, jax.ShapeDtypeStruct((2 * BLOCKS, BLOCKS, freqs), jnp.float32), [sums])
    csd = csd.reshape(2, BLOCKS, BLOCKS, freqs)
    return (spectra, jnp.transpose(csd, (0, 3, 1, 2)))


def solution(mesh):
    across = min(4, mesh.shape["space"] // 2)
    split = Mesh(mesh.devices.reshape(-1, across, 2, mesh.shape["blk"]), (*SPACE, "blk"))
    return jax.shard_map(
        local,
        mesh=split,
        in_specs=(P("blk", SPACE), P(None, SPACE), P(SPACE)),
        out_specs=(P(None, "blk", None, SPACE), P(None, "blk", None, None)),
        check_vma=False,
    )
```

```python
import functools
import math

import jax
import jax.numpy as jnp
import numpy as np
from jax import lax
from jax.experimental import pallas as pl
from jax.experimental.pallas import tpu as pltpu
from jax.sharding import Mesh
from jax.sharding import PartitionSpec as P

HOP = 128
BLEN = 2 * HOP
BLOCKS = 4
SPACE = ("z", "x", "core")
LIMIT = 16 * 1024 * 1024
WAIT = pl.CostEstimate(flops=10**10, bytes_accessed=10**10, transcendentals=0)
MEANS = 16
PAIRS = [(i, j) for i in range(BLOCKS) for j in range(i, BLOCKS)]
CROSS = [(i, j) for i, j in PAIRS if i < j]
SUMS = len(PAIRS) + len(CROSS)

VMEM = pl.BlockSpec(memory_space=pltpu.VMEM)
SMEM = pl.BlockSpec(memory_space=pltpu.SMEM)
HBM = pl.BlockSpec(memory_space=pltpu.HBM)
ANY = pl.BlockSpec(memory_space=pl.ANY)


def tables():
    t = np.arange(BLEN)
    k = np.arange(HOP)
    angle = 2.0 * math.pi / BLEN * (k[:, None] * t[None, :] % BLEN)
    scale = 1.0 / math.sqrt(3.0 * BLEN / 8.0)
    parts = np.stack([np.cos(angle) * scale, -np.sin(angle) * scale], axis=1)
    return (
        jnp.asarray(parts.reshape(2 * HOP, BLEN), jnp.bfloat16),
        jnp.asarray(parts.swapaxes(0, 1).reshape(2 * HOP, BLEN), jnp.bfloat16),
    )


def split_kernel(pressure_ref, out_ref, held, ready, sem_in, sem_out):
    width = out_ref.shape[2]

    def fetch(quarter):
        cols = slice(quarter * width, (quarter + 1) * width)
        return pltpu.make_async_copy(pressure_ref.at[:, cols], held.at[quarter], sem_in.at[quarter])

    def store(quarter):
        return pltpu.make_async_copy(ready.at[quarter], out_ref.at[quarter], sem_out.at[quarter])

    for quarter in range(BLOCKS):
        fetch(quarter).start()
    for quarter in range(BLOCKS):
        fetch(quarter).wait()
        x = held[quarter]
        mean = jnp.sum(x, axis=0, keepdims=True) * (1.0 / HOP)
        ready[quarter, :HOP] = (x - mean).astype(jnp.bfloat16)
        high = mean.astype(jnp.bfloat16).astype(jnp.float32)
        middle = (mean - high).astype(jnp.bfloat16).astype(jnp.float32)
        low = mean - high - middle
        row = lax.broadcasted_iota(jnp.int32, (MEANS, width), 0)
        rows = jnp.where(row == 0, high, jnp.where(row == 1, middle, jnp.where(row == 2, low, 0.0)))
        ready[quarter, HOP:] = rows.astype(jnp.bfloat16)
        store(quarter).start()
    for quarter in range(BLOCKS):
        store(quarter).wait()


def window():
    t = lax.broadcasted_iota(jnp.int32, (BLEN, 128), 0).astype(jnp.float32)
    square = ((t - HOP) * (math.pi / BLEN)) ** 2
    cosine = jnp.full_like(square, 1.0 / math.factorial(12))
    for order in range(10, -1, -2):
        cosine = cosine * square + (-1.0) ** (order // 2) / math.factorial(order)
    return cosine * cosine


def windows(segments, final, hann):
    means = [jnp.sum(ref[HOP:].astype(jnp.float32), axis=0, keepdims=True) for ref in segments]
    total = jnp.sum(final, axis=0, keepdims=True) + HOP * (means[0] + means[1] + means[2] + means[3])
    mean = total / (HOP * (BLOCKS + 1))
    hann = jnp.concatenate([hann] * (final.shape[1] // 128), axis=1)

    def segment(s):
        if s == BLOCKS:
            return final - mean
        return segments[s][:HOP].astype(jnp.float32) + (means[s] - mean)

    blocks = []
    for b in range(BLOCKS):
        windowed = jnp.concatenate([segment(b) * hann[:HOP], segment(b + 1) * hann[HOP:]], axis=0)
        blocks.append(windowed.astype(jnp.bfloat16))
    return blocks


def sums_kernel(
    count, pos_ref, got_ref, final_ref, weights_ref, table_ref, out_ref, coeff, sums, rows
):
    me = pos_ref[0]
    width = got_ref.shape[2]
    own = pl.ds(pl.multiple_of(me * width, width), width)
    segments = [got_ref.at[s] for s in range(BLOCKS)]
    for b, windowed in enumerate(windows(segments, final_ref[:, own], window())):
        apart = jnp.dot(table_ref[...], windowed, preferred_element_type=jnp.float32)
        coeff[b] = apart.astype(jnp.bfloat16).astype(jnp.float32)

    weights = weights_ref[:, own] * (1.0 / count)
    freqs = HOP // BLOCKS

    def tile(t, carry):
        at = pl.multiple_of(t * 8, 8)
        acc = [None] * SUMS
        for lane in range(0, width, 128):
            cols = slice(lane, lane + 128)
            w = weights[:, cols]
            re = [coeff[b, pl.ds(at, 8), cols] for b in range(BLOCKS)]
            im = [coeff[b, pl.ds(at + HOP, 8), cols] for b in range(BLOCKS)]
            re_w = [v * w for v in re]
            im_w = [v * w for v in im]
            terms = [re_w[i] * re[j] + im_w[i] * im[j] for i, j in PAIRS]
            terms += [im_w[i] * re[j] - re_w[i] * im[j] for i, j in CROSS]
            acc = [v if a is None else a + v for a, v in zip(acc, terms)]
        first = (t // (freqs // 8)) * (SUMS * freqs) + lax.rem(t, freqs // 8) * 8
        for p in range(SUMS):
            sums[pl.ds(pl.multiple_of(first + p * freqs, 8), 8), :] = acc[p]
        return carry

    lax.fori_loop(0, HOP // 8, tile, 0)
    ones = jnp.ones((8, 128), jnp.bfloat16)
    along = (((1,), (1,)), ((), ()))
    lanes = lax.dot_general(ones, sums[...].astype(jnp.bfloat16), along, preferred_element_type=jnp.float32)
    for row in range(rows.shape[0]):
        rows[row : row + 1] = lanes[:1, row * 128 : (row + 1) * 128]
    value = rows[...].astype(jnp.bfloat16)
    for copy in range(out_ref.shape[0]):
        out_ref[copy] = value


def fan_kernel(steps, pos_ref, sent_ref, *refs):
    *outs, sems = refs[len(refs) - len(steps) - 1 :]
    me = pos_ref[0]
    copies = []
    for at, (step, out) in enumerate(zip(steps, outs)):
        for place in range(BLOCKS - 1):
            quarter = lax.rem(me + step + 1 + place, BLOCKS)
            copies.append(pltpu.make_async_copy(sent_ref.at[quarter], out.at[place], sems.at[at, place]))
    for copy in copies:
        copy.start()
    for copy in copies:
        copy.wait()


def spectra_kernel(
    pos_ref, after_ref, final_ref, table_ref, own_ref, got_ref, got1, got2, got3, out_ref, token_ref, held, last, ready, sems, last_sems, out_sems
):
    me = pos_ref[0]
    width = own_ref.shape[2]
    own = BLOCKS - 1
    hann = window()

    def cols(place):
        return pl.ds(pl.multiple_of(lax.rem(me + 1 + place, BLOCKS) * width, width), width)

    fetches = []
    for place in range(BLOCKS):
        copies = [pltpu.make_async_copy(final_ref.at[:, cols(place)], last.at[place], last_sems.at[place])]
        if place == own:
            copies.append(pltpu.make_async_copy(got_ref, held.at[place], sems.at[place, 0]))
        else:
            mine = own_ref.at[lax.rem(me + 1 + place, BLOCKS)]
            copies.append(pltpu.make_async_copy(mine, held.at[place, me], sems.at[place, 0]))
            for step, got in enumerate((got1, got2, got3), 1):
                source = lax.rem(me + BLOCKS - step, BLOCKS)
                copies.append(
                    pltpu.make_async_copy(got.at[place], held.at[place, source], sems.at[place, step])
                )
        fetches.append(copies)
    stores = [
        pltpu.make_async_copy(ready.at[place], out_ref.at[:, :, :, cols(place)], out_sems.at[place])
        for place in range(BLOCKS)
    ]
    order = [own, *range(own)]
    for place in order:
        for copy in fetches[place]:
            copy.start()
    group = 2 * HOP // BLOCKS
    table = table_ref[pl.ds(pl.multiple_of(me * group, group), group), :]
    for place in order:
        for copy in fetches[place]:
            copy.wait()
        blocks = windows([held.at[place, s] for s in range(BLOCKS)], last[place], hann)
        for b, windowed in enumerate(blocks):
            mixed = jnp.dot(table, windowed, preferred_element_type=jnp.float32)
            ready[place, b] = mixed.astype(jnp.bfloat16).reshape(ready.shape[2:])
        stores[place].start()
    token_ref[...] = jnp.zeros_like(token_ref)
    for place in order:
        stores[place].wait()


def token_kernel(first_ref, second_ref, token_ref):
    token_ref[...] = jnp.zeros_like(token_ref)


def share_kernel(got_ref, out_ref):
    total = jnp.sum(got_ref[...].astype(jnp.float32), axis=0)
    part = total.shape[0] // BLOCKS
    copies = out_ref.shape[0] // BLOCKS
    for q in range(BLOCKS):
        for copy in range(copies):
            out_ref[q * copies + copy] = total[q * part : (q + 1) * part].astype(out_ref.dtype)


def matrix_kernel(got_ref, csd_ref):
    freqs = csd_ref.shape[2]
    total = jnp.sum(got_ref[...].astype(jnp.float32), axis=0)
    each = 128 // freqs
    rows = [total[p // each : p // each + 1, p % each * freqs : (p % each + 1) * freqs] for p in range(SUMS)]
    for i in range(BLOCKS):
        for j in range(BLOCKS):
            pair = (min(i, j), max(i, j))
            csd_ref[i, j : j + 1] = rows[PAIRS.index(pair)]
            if i == j:
                csd_ref[BLOCKS + i, j : j + 1] = jnp.zeros_like(rows[0])
            else:
                cross = rows[len(PAIRS) + CROSS.index(pair)]
                csd_ref[BLOCKS + i, j : j + 1] = cross if i < j else -cross


def call(kernel, out, operands, scratch=(), cost=None, out_spec=VMEM, limit=LIMIT):
    specs = [o[1] if isinstance(o, tuple) else VMEM for o in operands]
    return pl.pallas_call(
        kernel,
        out_shape=out,
        in_specs=specs,
        out_specs=out_spec,
        scratch_shapes=scratch,
        compiler_params=pltpu.CompilerParams(vmem_limit_bytes=limit),
        cost_estimate=cost,
    )(*[o[0] if isinstance(o, tuple) else o for o in operands])


def late_first(size):
    return [(i + size // 2 + 3) % size for i in range(size)]


def local(pressure, final_steps, weights):
    points = pressure.shape[1]
    width = points // BLOCKS
    freqs = HOP // BLOCKS
    here = (lax.axis_index("blk").astype(jnp.int32).reshape(1), SMEM)
    table, apart = tables()
    sent = pl.pallas_call(
        split_kernel,
        out_shape=jax.ShapeDtypeStruct((BLOCKS, HOP + MEANS, width), jnp.bfloat16),
        in_specs=[HBM],
        out_specs=HBM,
        scratch_shapes=[
            pltpu.VMEM((BLOCKS, HOP, width), jnp.float32),
            pltpu.VMEM((BLOCKS, HOP + MEANS, width), jnp.bfloat16),
            pltpu.SemaphoreType.DMA((BLOCKS,)),
            pltpu.SemaphoreType.DMA((BLOCKS,)),
        ],
        compiler_params=pltpu.CompilerParams(vmem_limit_bytes=60 * 1024 * 1024),
    )(pressure)
    got = lax.all_to_all(sent, "blk", 0, 0, tiled=True)
    part = jax.ShapeDtypeStruct((BLOCKS - 1, HOP + MEANS, width), jnp.bfloat16)

    def passed_on(steps, near):
        parts = call(
            functools.partial(fan_kernel, steps),
            [part] * len(steps),
            [here, (sent, ANY), *near],
            [pltpu.SemaphoreType.DMA((len(steps), BLOCKS - 1))],
            out_spec=[HBM] * len(steps),
        )
        return [
            lax.ppermute(value, "blk", [(i, (i + step) % BLOCKS) for i in range(BLOCKS)])
            for step, value in zip(steps, parts)
        ]

    moved = passed_on((1,), [apart, weights.reshape(1, points), table]) + passed_on((2,), []) + passed_on((3,), [])

    group = ("blk", "x", "core")
    count = float(points * lax.axis_size(SPACE))
    lines = SUMS * HOP // 128
    sums = call(
        functools.partial(sums_kernel, count),
        jax.ShapeDtypeStruct((lax.axis_size("z"), lines, 128), jnp.bfloat16),
        [here, got, final_steps, weights.reshape(1, points), apart],
        [
            pltpu.VMEM((BLOCKS, 2 * HOP, width), jnp.float32),
            pltpu.VMEM((SUMS * HOP, 128), jnp.float32),
            pltpu.VMEM((lines, 128), jnp.float32),
        ],
        cost=WAIT,
    )
    sums = lax.all_to_all(sums, "z", 0, 0, tiled=True, axis_index_groups=[late_first(lax.axis_size("z"))])
    token = jax.ShapeDtypeStruct((8, 128), jnp.float32)
    after = call(
        token_kernel, token, [(moved[0], ANY), (moved[1], ANY)], cost=WAIT
    )
    spectra, token = call(
        spectra_kernel,
        [jax.ShapeDtypeStruct((BLOCKS, freqs, 2, points), jnp.bfloat16), token],
        [here, after, (final_steps, ANY), table, (sent, ANY), (got, ANY), *((value, ANY) for value in moved)],
        [
            pltpu.VMEM((BLOCKS, BLOCKS, HOP + MEANS, width), jnp.bfloat16),
            pltpu.VMEM((BLOCKS, HOP, width), jnp.float32),
            pltpu.VMEM((BLOCKS, BLOCKS, freqs, 2, width), jnp.bfloat16),
            pltpu.SemaphoreType.DMA((BLOCKS, BLOCKS)),
            pltpu.SemaphoreType.DMA((BLOCKS,)),
            pltpu.SemaphoreType.DMA((BLOCKS,)),
        ],
        out_spec=[ANY, VMEM],
    )
    shares = jax.ShapeDtypeStruct((lax.axis_size(group), lines // BLOCKS, 128), jnp.bfloat16)
    sums = lax.all_to_all(call(share_kernel, shares, [sums]), group, 0, 0, tiled=True)
    csd = call(matrix_kernel, jax.ShapeDtypeStruct((2 * BLOCKS, BLOCKS, freqs), jnp.float32), [sums])
    csd = csd.reshape(2, BLOCKS, BLOCKS, freqs)
    return (spectra, jnp.transpose(csd, (0, 3, 1, 2)))


def solution(mesh):
    across = min(4, mesh.shape["space"] // 2)
    split = Mesh(mesh.devices.reshape(-1, across, 2, mesh.shape["blk"]), (*SPACE, "blk"))
    return jax.shard_map(
        local,
        mesh=split,
        in_specs=(P("blk", SPACE), P(None, SPACE), P(SPACE)),
        out_specs=(P(None, "blk", None, SPACE), P(None, "blk", None, None)),
        check_vma=False,
    )
```

```python
import functools
import math

import jax
import jax.numpy as jnp
import numpy as np
from jax import lax
from jax.experimental import pallas as pl
from jax.experimental.pallas import tpu as pltpu
from jax.sharding import Mesh
from jax.sharding import PartitionSpec as P

HOP = 128
BLEN = 2 * HOP
BLOCKS = 4
SPACE = ("z", "x", "core")
LIMIT = 16 * 1024 * 1024
WAIT = pl.CostEstimate(flops=10**10, bytes_accessed=10**10, transcendentals=0)
MEANS = 16
PAIRS = [(i, j) for i in range(BLOCKS) for j in range(i, BLOCKS)]
CROSS = [(i, j) for i, j in PAIRS if i < j]
SUMS = len(PAIRS) + len(CROSS)

VMEM = pl.BlockSpec(memory_space=pltpu.VMEM)
SMEM = pl.BlockSpec(memory_space=pltpu.SMEM)
HBM = pl.BlockSpec(memory_space=pltpu.HBM)
ANY = pl.BlockSpec(memory_space=pl.ANY)


def tables():
    t = np.arange(BLEN)
    k = np.arange(HOP)
    angle = 2.0 * math.pi / BLEN * (k[:, None] * t[None, :] % BLEN)
    scale = 1.0 / math.sqrt(3.0 * BLEN / 8.0)
    parts = np.stack([np.cos(angle) * scale, -np.sin(angle) * scale], axis=1)
    return (
        jnp.asarray(parts.reshape(2 * HOP, BLEN), jnp.bfloat16),
        jnp.asarray(parts.swapaxes(0, 1).reshape(2 * HOP, BLEN), jnp.bfloat16),
    )


def split_kernel(pressure_ref, out_ref, held, ready, sem_in, sem_out):
    width = out_ref.shape[2]

    def fetch(quarter):
        cols = slice(quarter * width, (quarter + 1) * width)
        return pltpu.make_async_copy(pressure_ref.at[:, cols], held.at[quarter], sem_in.at[quarter])

    def store(quarter):
        return pltpu.make_async_copy(ready.at[quarter], out_ref.at[quarter], sem_out.at[quarter])

    for quarter in range(BLOCKS):
        fetch(quarter).start()
    for quarter in range(BLOCKS):
        fetch(quarter).wait()
        x = held[quarter]
        mean = jnp.sum(x, axis=0, keepdims=True) * (1.0 / HOP)
        ready[quarter, :HOP] = (x - mean).astype(jnp.bfloat16)
        high = mean.astype(jnp.bfloat16).astype(jnp.float32)
        middle = (mean - high).astype(jnp.bfloat16).astype(jnp.float32)
        low = mean - high - middle
        row = lax.broadcasted_iota(jnp.int32, (MEANS, width), 0)
        rows = jnp.where(row == 0, high, jnp.where(row == 1, middle, jnp.where(row == 2, low, 0.0)))
        ready[quarter, HOP:] = rows.astype(jnp.bfloat16)
        store(quarter).start()
    for quarter in range(BLOCKS):
        store(quarter).wait()


def window():
    t = lax.broadcasted_iota(jnp.int32, (BLEN, 128), 0).astype(jnp.float32)
    square = ((t - HOP) * (math.pi / BLEN)) ** 2
    cosine = jnp.full_like(square, 1.0 / math.factorial(12))
    for order in range(10, -1, -2):
        cosine = cosine * square + (-1.0) ** (order // 2) / math.factorial(order)
    return cosine * cosine


def windows(segments, final, hann):
    means = [jnp.sum(ref[HOP:].astype(jnp.float32), axis=0, keepdims=True) for ref in segments]
    total = jnp.sum(final, axis=0, keepdims=True) + HOP * (means[0] + means[1] + means[2] + means[3])
    mean = total / (HOP * (BLOCKS + 1))
    hann = jnp.concatenate([hann] * (final.shape[1] // 128), axis=1)

    def segment(s):
        if s == BLOCKS:
            return final - mean
        return segments[s][:HOP].astype(jnp.float32) + (means[s] - mean)

    blocks = []
    for b in range(BLOCKS):
        windowed = jnp.concatenate([segment(b) * hann[:HOP], segment(b + 1) * hann[HOP:]], axis=0)
        blocks.append(windowed.astype(jnp.bfloat16))
    return blocks


def sums_kernel(
    count, pos_ref, got_ref, final_ref, weights_ref, table_ref, out_ref, coeff, sums, rows
):
    me = pos_ref[0]
    width = got_ref.shape[2]
    own = pl.ds(pl.multiple_of(me * width, width), width)
    segments = [got_ref.at[s] for s in range(BLOCKS)]
    for b, windowed in enumerate(windows(segments, final_ref[:, own], window())):
        apart = jnp.dot(table_ref[...], windowed, preferred_element_type=jnp.float32)
        coeff[b] = apart.astype(jnp.bfloat16).astype(jnp.float32)

    weights = weights_ref[:, own] * (1.0 / count)
    freqs = HOP // BLOCKS

    def tile(t, carry):
        at = pl.multiple_of(t * 8, 8)
        acc = [None] * SUMS
        for lane in range(0, width, 128):
            cols = slice(lane, lane + 128)
            w = weights[:, cols]
            re = [coeff[b, pl.ds(at, 8), cols] for b in range(BLOCKS)]
            im = [coeff[b, pl.ds(at + HOP, 8), cols] for b in range(BLOCKS)]
            re_w = [v * w for v in re]
            im_w = [v * w for v in im]
            terms = [re_w[i] * re[j] + im_w[i] * im[j] for i, j in PAIRS]
            terms += [im_w[i] * re[j] - re_w[i] * im[j] for i, j in CROSS]
            acc = [v if a is None else a + v for a, v in zip(acc, terms)]
        first = (t // (freqs // 8)) * (SUMS * freqs) + lax.rem(t, freqs // 8) * 8
        for p in range(SUMS):
            sums[pl.ds(pl.multiple_of(first + p * freqs, 8), 8), :] = acc[p]
        return carry

    lax.fori_loop(0, HOP // 8, tile, 0)
    ones = jnp.ones((8, 128), jnp.bfloat16)
    along = (((1,), (1,)), ((), ()))
    lanes = lax.dot_general(ones, sums[...].astype(jnp.bfloat16), along, preferred_element_type=jnp.float32)
    for row in range(rows.shape[0]):
        rows[row : row + 1] = lanes[:1, row * 128 : (row + 1) * 128]
    value = rows[...].astype(jnp.bfloat16)
    for copy in range(out_ref.shape[0]):
        out_ref[copy] = value


def fan_kernel(steps, pos_ref, sent_ref, *refs):
    *outs, sems = refs[len(refs) - len(steps) - 1 :]
    me = pos_ref[0]
    copies = []
    for at, (step, out) in enumerate(zip(steps, outs)):
        for place in range(BLOCKS - 1):
            quarter = lax.rem(me + step + 1 + place, BLOCKS)
            copies.append(pltpu.make_async_copy(sent_ref.at[quarter], out.at[place], sems.at[at, place]))
    for copy in copies:
        copy.start()
    for copy in copies:
        copy.wait()


def spectra_kernel(
    pos_ref, after_ref, final_ref, table_ref, own_ref, got_ref, got1, got2, got3, out_ref, token_ref, held, last, ready, sems, last_sems, out_sems
):
    me = pos_ref[0]
    width = own_ref.shape[2]
    own = BLOCKS - 1
    hann = window()

    def cols(place):
        return pl.ds(pl.multiple_of(lax.rem(me + 1 + place, BLOCKS) * width, width), width)

    fetches = []
    for place in range(BLOCKS):
        copies = [pltpu.make_async_copy(final_ref.at[:, cols(place)], last.at[place], last_sems.at[place])]
        if place == own:
            copies.append(pltpu.make_async_copy(got_ref, held.at[place], sems.at[place, 0]))
        else:
            mine = own_ref.at[lax.rem(me + 1 + place, BLOCKS)]
            copies.append(pltpu.make_async_copy(mine, held.at[place, me], sems.at[place, 0]))
            for step, got in enumerate((got1, got2, got3), 1):
                source = lax.rem(me + BLOCKS - step, BLOCKS)
                copies.append(
                    pltpu.make_async_copy(got.at[place], held.at[place, source], sems.at[place, step])
                )
        fetches.append(copies)
    stores = [
        pltpu.make_async_copy(ready.at[place], out_ref.at[:, :, :, cols(place)], out_sems.at[place])
        for place in range(BLOCKS)
    ]
    order = [own, *range(own)]
    for place in order:
        for copy in fetches[place]:
            copy.start()
    group = 2 * HOP // BLOCKS
    table = table_ref[pl.ds(pl.multiple_of(me * group, group), group), :]
    for place in order:
        for copy in fetches[place]:
            copy.wait()
        blocks = windows([held.at[place, s] for s in range(BLOCKS)], last[place], hann)
        for b, windowed in enumerate(blocks):
            mixed = jnp.dot(table, windowed, preferred_element_type=jnp.float32)
            ready[place, b] = mixed.astype(jnp.bfloat16).reshape(ready.shape[2:])
        stores[place].start()
    token_ref[...] = jnp.zeros_like(token_ref)
    for place in order:
        stores[place].wait()


def token_kernel(first_ref, second_ref, token_ref):
    token_ref[...] = jnp.zeros_like(token_ref)


def share_kernel(got_ref, out_ref):
    total = jnp.sum(got_ref[...].astype(jnp.float32), axis=0)
    part = total.shape[0] // BLOCKS
    copies = out_ref.shape[0] // BLOCKS
    for q in range(BLOCKS):
        for copy in range(copies):
            out_ref[q * copies + copy] = total[q * part : (q + 1) * part].astype(out_ref.dtype)


def matrix_kernel(got_ref, csd_ref):
    freqs = csd_ref.shape[2]
    total = jnp.sum(got_ref[...].astype(jnp.float32), axis=0)
    each = 128 // freqs
    rows = [total[p // each : p // each + 1, p % each * freqs : (p % each + 1) * freqs] for p in range(SUMS)]
    for i in range(BLOCKS):
        for j in range(BLOCKS):
            pair = (min(i, j), max(i, j))
            csd_ref[i, j : j + 1] = rows[PAIRS.index(pair)]
            if i == j:
                csd_ref[BLOCKS + i, j : j + 1] = jnp.zeros_like(rows[0])
            else:
                cross = rows[len(PAIRS) + CROSS.index(pair)]
                csd_ref[BLOCKS + i, j : j + 1] = cross if i < j else -cross


def call(kernel, out, operands, scratch=(), cost=None, out_spec=VMEM, limit=LIMIT):
    specs = [o[1] if isinstance(o, tuple) else VMEM for o in operands]
    return pl.pallas_call(
        kernel,
        out_shape=out,
        in_specs=specs,
        out_specs=out_spec,
        scratch_shapes=scratch,
        compiler_params=pltpu.CompilerParams(vmem_limit_bytes=limit),
        cost_estimate=cost,
    )(*[o[0] if isinstance(o, tuple) else o for o in operands])


def late_first(size):
    return [(i + size // 2 + 3) % size for i in range(size)]


def local(pressure, final_steps, weights):
    points = pressure.shape[1]
    width = points // BLOCKS
    freqs = HOP // BLOCKS
    here = (lax.axis_index("blk").astype(jnp.int32).reshape(1), SMEM)
    table, apart = tables()
    sent = pl.pallas_call(
        split_kernel,
        out_shape=jax.ShapeDtypeStruct((BLOCKS, HOP + MEANS, width), jnp.bfloat16),
        in_specs=[HBM],
        out_specs=HBM,
        scratch_shapes=[
            pltpu.VMEM((BLOCKS, HOP, width), jnp.float32),
            pltpu.VMEM((BLOCKS, HOP + MEANS, width), jnp.bfloat16),
            pltpu.SemaphoreType.DMA((BLOCKS,)),
            pltpu.SemaphoreType.DMA((BLOCKS,)),
        ],
        compiler_params=pltpu.CompilerParams(vmem_limit_bytes=60 * 1024 * 1024),
    )(pressure)
    got = lax.all_to_all(sent, "blk", 0, 0, tiled=True)
    part = jax.ShapeDtypeStruct((BLOCKS - 1, HOP + MEANS, width), jnp.bfloat16)

    def passed_on(steps, near):
        parts = call(
            functools.partial(fan_kernel, steps),
            [part] * len(steps),
            [here, (sent, ANY), *near],
            [pltpu.SemaphoreType.DMA((len(steps), BLOCKS - 1))],
            out_spec=[HBM] * len(steps),
        )
        return [
            lax.ppermute(value, "blk", [(i, (i + step) % BLOCKS) for i in range(BLOCKS)])
            for step, value in zip(steps, parts)
        ]

    two_on = passed_on((2,), [apart, weights.reshape(1, points), table])
    moved = passed_on((1,), []) + two_on + passed_on((3,), [])

    group = ("blk", "x", "core")
    count = float(points * lax.axis_size(SPACE))
    lines = SUMS * HOP // 128
    sums = call(
        functools.partial(sums_kernel, count),
        jax.ShapeDtypeStruct((lax.axis_size("z"), lines, 128), jnp.bfloat16),
        [here, got, final_steps, weights.reshape(1, points), apart],
        [
            pltpu.VMEM((BLOCKS, 2 * HOP, width), jnp.float32),
            pltpu.VMEM((SUMS * HOP, 128), jnp.float32),
            pltpu.VMEM((lines, 128), jnp.float32),
        ],
        cost=WAIT,
    )
    sums = lax.all_to_all(sums, "z", 0, 0, tiled=True, axis_index_groups=[late_first(lax.axis_size("z"))])
    token = jax.ShapeDtypeStruct((8, 128), jnp.float32)
    after = call(
        token_kernel, token, [(moved[0], ANY), (moved[1], ANY)], cost=WAIT
    )
    spectra, token = call(
        spectra_kernel,
        [jax.ShapeDtypeStruct((BLOCKS, freqs, 2, points), jnp.bfloat16), token],
        [here, after, (final_steps, ANY), table, (sent, ANY), (got, ANY), *((value, ANY) for value in moved)],
        [
            pltpu.VMEM((BLOCKS, BLOCKS, HOP + MEANS, width), jnp.bfloat16),
            pltpu.VMEM((BLOCKS, HOP, width), jnp.float32),
            pltpu.VMEM((BLOCKS, BLOCKS, freqs, 2, width), jnp.bfloat16),
            pltpu.SemaphoreType.DMA((BLOCKS, BLOCKS)),
            pltpu.SemaphoreType.DMA((BLOCKS,)),
            pltpu.SemaphoreType.DMA((BLOCKS,)),
        ],
        out_spec=[ANY, VMEM],
    )
    shares = jax.ShapeDtypeStruct((lax.axis_size(group), lines // BLOCKS, 128), jnp.bfloat16)
    sums = lax.all_to_all(call(share_kernel, shares, [sums]), group, 0, 0, tiled=True)
    csd = call(matrix_kernel, jax.ShapeDtypeStruct((2 * BLOCKS, BLOCKS, freqs), jnp.float32), [sums])
    csd = csd.reshape(2, BLOCKS, BLOCKS, freqs)
    return (spectra, jnp.transpose(csd, (0, 3, 1, 2)))


def solution(mesh):
    across = min(4, mesh.shape["space"] // 2)
    split = Mesh(mesh.devices.reshape(-1, across, 2, mesh.shape["blk"]), (*SPACE, "blk"))
    return jax.shard_map(
        local,
        mesh=split,
        in_specs=(P("blk", SPACE), P(None, SPACE), P(SPACE)),
        out_specs=(P(None, "blk", None, SPACE), P(None, "blk", None, None)),
        check_vma=False,
    )
```
